512 devices in a mesh: seq: 128 (over y, z, x_lo), head: 4 (over x_hi, core).
Axes of the slice: x: 4 (x_hi: 2, x_lo: 2; x = x_hi * 2 + x_lo), y: 4, z: 16, core: 2. Of those that a mesh axis runs over, the one named last changes fastest.
Arguments:
- queries: bfloat16 [32768, 8192], P('seq', 'head'), may hold values from -40 to 40
- key_rows: bfloat16 [32768, 8192], P('seq', 'head'), may hold values from -20 to 20
- value_rows: bfloat16 [32768, 8192], P('seq', 'head'), may hold values from -8 to 8
Outputs:
- attended: bfloat16 [32768, 8192], P('seq', 'head')
The draws below stay inside these ranges and needn't reach their ends.
All inputs are finite; a program needn't handle non-finite values.
Results may differ from the reference program's by a relative error of at most 0.0043.
Values may be sent and summed in bfloat16 or wider, within the bound.
No kernel may reach another device: no remote copies, remote signals or barrier semaphores. Data moves between devices by JAX's collectives and lax.ppermute only.
A program may use at most 128 MiB of HBM per device.

```python
import math
from functools import reduce
import jax
import jax.numpy as jnp
from jax import lax

HEADS = 64
HEAD_DIM = 128
BLOCK = 128
POOL = 64
MID_REACH = 3
FAR_REACH = 9
TOKENS = 32768


def rough_field(folded, rows_total):
    return jax.random.truncated_normal(folded, -4.0, 4.0, (rows_total, HEADS * HEAD_DIM), jnp.float32)


def group_field(folded):
    group_part = jax.random.truncated_normal(folded, -4.0, 4.0, (TOKENS // POOL, HEADS * HEAD_DIM), jnp.float32)
    return jnp.repeat(group_part, POOL, axis=0)


def paired_keys(key):
    folded = jax.random.fold_in(key, 11)
    drawn = 3.0 * rough_field(jax.random.fold_in(folded, 1), TOKENS) + 1.5 * group_field(jax.random.fold_in(folded, 2))
    return drawn


def draw_key_rows(key, part):
    return paired_keys(key).astype(jnp.bfloat16)


def draw_queries(key, part):
    drawn = rough_field(jax.random.fold_in(key, 23), TOKENS)
    return drawn.astype(jnp.bfloat16)


def draw_value_rows(key, part):
    folded = jax.random.fold_in(key, 31)
    drawn = rough_field(jax.random.fold_in(folded, 1), TOKENS) + group_field(jax.random.fold_in(folded, 2))
    return drawn.astype(jnp.bfloat16)


def setup_inputs(seed: int = 0) -> dict:
    key_list = jax.random.split(jax.random.key(seed), 4)
    return {
        "queries": draw_queries(jax.random.fold_in(key_list[3], 71), 0),
        "key_rows": draw_key_rows(jax.random.fold_in(key_list[3], 71), 0),
        "value_rows": draw_value_rows(jax.random.fold_in(key_list[3], 71), 0),
    }


def pool_pairs(source):
    paired = source.astype(jnp.float32).reshape(source.shape[0] // 2, 2, source.shape[1])
    return (0.5 * (paired[:, 0] + paired[:, 1])).astype(jnp.bfloat16)

def pool_groups(source, group_rows):
    grouped = source.astype(jnp.float32).reshape(source.shape[0] // group_rows, group_rows, source.shape[1])
    return lax.optimization_barrier(jnp.mean(grouped, axis=1)).astype(jnp.bfloat16)

def padded(source, margin):
    return jnp.pad(source, ((margin, margin), (0, 0)))

def as_heads(source):
    return source.astype(jnp.float32).reshape(source.shape[0], HEADS, HEAD_DIM)

def reference(queries, key_rows, value_rows):
    score_scale = 1.0 / math.sqrt(HEAD_DIM)
    key_two = pool_pairs(key_rows)
    value_two = pool_pairs(value_rows)
    key_four = pool_pairs(key_two)
    value_four = pool_pairs(value_two)
    key_coarse = pool_groups(key_four, POOL // 4)
    value_coarse = pool_groups(value_four, POOL // 4)
    half_rows = BLOCK // 2
    quarter = BLOCK // 4
    blocks_all = TOKENS // BLOCK
    fine_pads = (padded(key_rows, BLOCK), padded(value_rows, BLOCK))
    mid_pads = (padded(key_two, MID_REACH * half_rows), padded(value_two, MID_REACH * half_rows))
    far_pads = (padded(key_four, FAR_REACH * quarter), padded(value_four, FAR_REACH * quarter))
    coarse_block = POOL * jnp.arange(TOKENS // POOL, dtype=jnp.int32) // BLOCK
    fine_span = 3 * BLOCK
    mid_span = (2 * MID_REACH + 1) * half_rows
    far_span = (2 * FAR_REACH + 1) * quarter

    def window(pads, anchor, span):
        return (lax.dynamic_slice_in_dim(pads[0], anchor, span, 0), lax.dynamic_slice_in_dim(pads[1], anchor, span, 0))

    def one_block(block_index):
        query_rows = as_heads(lax.dynamic_slice_in_dim(queries, block_index * BLOCK, BLOCK, 0))
        fine_pair = window(fine_pads, block_index * BLOCK, fine_span)
        mid_pair = window(mid_pads, block_index * half_rows, mid_span)
        far_pair = window(far_pads, block_index * quarter, far_span)
        fine_block = block_index - 1 + jnp.arange(fine_span, dtype=jnp.int32) // BLOCK
        mid_block = block_index - MID_REACH + jnp.arange(mid_span, dtype=jnp.int32) // half_rows
        far_block = block_index - FAR_REACH + jnp.arange(far_span, dtype=jnp.int32) // quarter
        level_list = [(fine_pair, fine_block, 0, 1, 0.0), (mid_pair, mid_block, 2, MID_REACH, math.log(2.0)), (far_pair, far_block, MID_REACH + 1, FAR_REACH, math.log(4.0)), ((key_coarse, value_coarse), coarse_block, FAR_REACH + 1, blocks_all, math.log(POOL))]
        score_list = []
        for pair_rows, atom_block, lowest, highest, log_size in level_list:
            gap_blocks = jnp.abs(atom_block - block_index)
            allowed = (atom_block >= 0) & (atom_block < blocks_all) & (gap_blocks >= lowest) & (gap_blocks <= highest)
            scores = jnp.einsum('qhe,khe->hqk', query_rows, as_heads(pair_rows[0])) * score_scale + log_size
            score_list.append(jnp.where(allowed[None, None, :], scores, -jnp.inf))
        row_top = reduce(jnp.maximum, [lax.optimization_barrier(jnp.max(scores, axis=2)) for scores in score_list])
        denominator = jnp.zeros((HEADS, BLOCK), jnp.float32)
        weighted = jnp.zeros((BLOCK, HEADS, HEAD_DIM), jnp.float32)
        for scores, level_item in zip(score_list, level_list):
            exp_terms = jnp.exp(scores - row_top[:, :, None])
            denominator = denominator + lax.optimization_barrier(jnp.sum(exp_terms, axis=2))
            rounded = lax.optimization_barrier(exp_terms.astype(jnp.bfloat16))
            weighted = weighted + jnp.einsum('hqk,khe->qhe', rounded.astype(jnp.float32), as_heads(level_item[0][1]))
        result = weighted / jnp.transpose(denominator)[:, :, None]
        return result.reshape(BLOCK, HEADS * HEAD_DIM).astype(jnp.bfloat16)
    blocks = lax.map(one_block, jnp.arange(blocks_all, dtype=jnp.int32))
    return blocks.reshape(TOKENS, HEADS * HEAD_DIM)
```

```python
import functools
import math

import jax
import jax.numpy as jnp
from jax import lax
from jax.experimental import pallas as pl
from jax.experimental.pallas import tpu as pltpu
from jax.sharding import Mesh
from jax.sharding import PartitionSpec as P

D = 128
BLOCK = 128
FAR_REACH = 9
SEQ = ("y", "z", "xl")
YZ = ("y", "z")
Z = "z"
BF = jnp.bfloat16
F32 = jnp.float32
SCALE = math.log2(math.e) / math.sqrt(D)


def halved(x, scratch):
    rows, cols = x.shape
    parts = []
    for c in range(cols // D):
        scratch[c, 0:rows] = x[:, c * D : (c + 1) * D]
        even = scratch[c, pl.ds(0, rows // 2, stride=2)]
        odd = scratch[c, pl.ds(1, rows // 2, stride=2)]
        parts.append((0.5 * (even + odd)).astype(BF))
    return parts[0] if len(parts) == 1 else jnp.concatenate(parts, axis=1)


def coarse_kernel(own_ref, send_ref, out_ref, scratch):
    pieces = []
    for ref in (own_ref, send_ref):
        four = halved(halved(ref[0].astype(F32), scratch).astype(F32), scratch)
        rows, cols = four.shape
        pieces.append(jnp.sum(four.astype(F32).reshape(rows // 16, 16, cols), axis=1) * (1.0 / 16))
    pieces.append(jnp.zeros((16 - 2 * (rows // 16), cols), F32))
    out_ref[0] = jnp.concatenate(pieces, axis=0).astype(BF)


def coarse_rows(own, send):
    _, rows, cols = own.shape
    width = 512
    return pl.pallas_call(
        coarse_kernel,
        grid=(2, cols // width),
        in_specs=[pl.BlockSpec((1, rows, width), lambda i, c: (i, 0, c))] * 2,
        out_specs=pl.BlockSpec((1, 16, width), lambda i, c: (i, 0, c)),
        out_shape=jax.ShapeDtypeStruct((2, 16, cols), BF),
        scratch_shapes=[pltpu.VMEM((width // D, rows, D), F32)],
        cost_estimate=pl.CostEstimate(flops=rows * cols * 8, bytes_accessed=8 * rows * cols, transcendentals=0),
    )(own, send)


def pool_kernel(own_ref, got_ref, up_ref, down_ref, mid_ref, far_ref, scratch):
    low = lax.axis_index("xl") == 0
    first = jnp.where(low, own_ref[0], got_ref[0])
    second = jnp.where(low, got_ref[0], own_ref[0])
    mid_first = halved(first.astype(F32), scratch)
    mid_second = halved(second.astype(F32), scratch)
    far_first = halved(mid_first.astype(F32), scratch)
    far_second = halved(mid_second.astype(F32), scratch)
    mid_ref[0, 0:128] = mid_first
    mid_ref[0, 128:256] = mid_second
    far_ref[0, 0:64] = far_first
    far_ref[0, 64:128] = far_second
    up_ref[0, 0:128] = second[128:256]
    up_ref[0, 128:192] = mid_first[64:128]
    up_ref[0, 192:256] = mid_second[0:64]
    up_ref[0, 256:288] = far_first[0:32]
    down_ref[0, 0:128] = first[0:128]
    down_ref[0, 128:192] = mid_first[64:128]
    down_ref[0, 192:256] = mid_second[0:64]
    down_ref[0, 256:288] = far_second[32:64]


def pooled(own, got):
    _, rows, cols = own.shape
    width = 512
    sizes = (288, 288, 256, 128)
    return pl.pallas_call(
        pool_kernel,
        grid=(2, cols // width),
        in_specs=[pl.BlockSpec((1, rows, width), lambda i, c: (i, 0, c))] * 2,
        out_specs=[pl.BlockSpec((1, n, width), lambda i, c: (i, 0, c)) for n in sizes],
        out_shape=[jax.ShapeDtypeStruct((2, n, cols), BF) for n in sizes],
        scratch_shapes=[pltpu.VMEM((width // D, rows, D), F32)],
        cost_estimate=pl.CostEstimate(flops=rows * cols * 8, bytes_accessed=16 * rows * cols, transcendentals=0),
    )(own, got)


def forward_kernel(below_ref, above_ref, up_ref, down_ref, near_ref, scratch):
    below, above = below_ref[0], above_ref[0]
    below_near = halved(below[0:128].astype(F32), scratch)
    above_near = halved(above[0:128].astype(F32), scratch)
    near_ref[0, 0:64] = below_near
    near_ref[0, 64:128] = above_near
    up_ref[0, 0:32] = below[256:288]
    up_ref[0, 32:128] = halved(jnp.concatenate([below[128:256], below_near], axis=0).astype(F32), scratch)
    down_ref[0, 0:96] = halved(jnp.concatenate([above_near, above[128:256]], axis=0).astype(F32), scratch)
    down_ref[0, 96:128] = above[256:288]


def forwarded(below, above):
    _, rows, cols = below.shape
    width = 512
    return pl.pallas_call(
        forward_kernel,
        grid=(2, cols // width),
        in_specs=[pl.BlockSpec((1, rows, width), lambda i, c: (i, 0, c))] * 2,
        out_specs=[pl.BlockSpec((1, 128, width), lambda i, c: (i, 0, c))] * 3,
        out_shape=[jax.ShapeDtypeStruct((2, 128, cols), BF)] * 3,
        scratch_shapes=[pltpu.VMEM((width // D, 192, D), F32)],
        cost_estimate=pl.CostEstimate(flops=2048 * cols, bytes_accessed=3000 * cols, transcendentals=0),
    )(below, above)


def attend_kernel(
    q_own, q_got, kv_own, kv_got, mid, far, below1, above1, up, down, near, below2, above2, below3, above3,
    coarse0, coarse1, coarse2, coarse3,
    own_out, send_out,
    kf, vf, km, vm, kr, vr, kc, vc, kfar, vfar, mask,
):
    low = lax.axis_index("xl") == 0
    y = lax.axis_index("y")
    ny, nz = lax.axis_size("y"), lax.axis_size(Z)
    zz = y * nz + lax.axis_index(Z)
    last = ny * nz - 1
    coarse_n = 4 * coarse0.shape[1]

    @pl.when(pl.program_id(0) == 0)
    def _():
        def flags(blocks, first, unit, ref):
            block = first + lax.broadcasted_iota(jnp.int32, (blocks * unit, D), 0) // unit + 4 * zz
            good = (block >= 0) & (block < 4 * (last + 1))
            ref[:, D : 2 * D] = jnp.where(good, 1.0, 0.0).astype(BF)

        flags(6, -1, 128, vf)
        flags(10, -3, 64, vm)
        flags(22, -9, 32, vr)
        vc[:, D : 2 * D] = jnp.ones((coarse_n, D), BF)
        for b in range(4):
            at = lax.broadcasted_iota(jnp.int32, (16, coarse_n), 1)
            turn = at // (8 * nz)
            other = (y + jnp.where(turn == 0, 0, jnp.where(turn == 1, ny - 1, jnp.where(turn == 2, 1, 2)))) % ny
            block = (other * nz + (at // 8) % nz) * 4 + (at % 8) // 2
            gap = jnp.abs(block - (4 * zz + b))
            mask[b * 16 : (b + 1) * 16, :] = jnp.where(gap > FAR_REACH, 1.0, 0.0).astype(BF)

    has = [zz >= n for n in range(4)]
    has_up = [zz <= last - n for n in range(4)]

    def pick(when_low, when_high, i, start, stop):
        return jnp.where(low, when_low[i, start:stop], when_high[i, start:stop])

    for i, (fine_w, mid_w, far_w) in enumerate(((kf, km, kr), (vf, vm, vr))):
        is_key = i == 0

        def put(ref, start, rows, present, fallback):
            n = rows.shape[0]
            ref[start : start + n, 0:D] = jnp.where(present, rows, fallback) if is_key else rows

        first, second = pick(kv_own, kv_got, i, 0, 256), pick(kv_got, kv_own, i, 0, 256)
        fine_w[128:384, 0:D] = first
        fine_w[384:640, 0:D] = second
        put(fine_w, 0, below1[i, 0:128], has[1], first[0:128])
        put(fine_w, 640, above1[i, 0:128], has_up[1], second[128:256])
        mid_w[192:448, 0:D] = mid[i]
        m0, m3 = mid[i, 0:64], mid[i, 192:256]
        put(mid_w, 0, below1[i, 128:192], has[1], m0)
        put(mid_w, 64, below1[i, 192:256], has[1], m0)
        put(mid_w, 128, near[i, 0:64], has[1], m0)
        put(mid_w, 448, near[i, 64:128], has_up[1], m3)
        put(mid_w, 512, above1[i, 128:192], has_up[1], m3)
        put(mid_w, 576, above1[i, 192:256], has_up[1], m3)
        far_w[288:416, 0:D] = far[i]
        f0, f3 = far[i, 0:32], far[i, 96:128]
        f0_4 = jnp.concatenate([f0] * 4, axis=0)
        f3_4 = jnp.concatenate([f3] * 4, axis=0)
        put(far_w, 0, below3[i], has[3], f0)
        put(far_w, 32, below2[i], has[2], f0_4)
        put(far_w, 160, up[i], has[1], f0_4)
        put(far_w, 416, down[i], has_up[1], f3_4)
        put(far_w, 544, above2[i], has_up[2], f3_4)
        put(far_w, 672, above3[i], has_up[3], f3)
    step = coarse_n // 4
    for t, part in enumerate((coarse0, coarse1, coarse2, coarse3)):
        kc[t * step : (t + 1) * step] = part[0]
        vc[t * step : (t + 1) * step, 0:D] = part[1]

    qo, qg = q_own[...], q_got[...]
    q_first = jnp.where(low, qo, qg)
    q_second = jnp.where(low, qg, qo)

    def scores(a, b):
        return lax.dot_general(a, b, (((1,), (1,)), ((), ())), preferred_element_type=F32)

    results = []
    for b in range(4):
        q = (q_first if b < 2 else q_second)[(b % 2) * 128 : (b % 2 + 1) * 128]
        kfar[0:192] = kr[b * 32 : b * 32 + 192]
        kfar[192:384] = kr[(b + 13) * 32 : (b + 13) * 32 + 192]
        vfar[0:192] = vr[b * 32 : b * 32 + 192]
        vfar[192:384] = vr[(b + 13) * 32 : (b + 13) * 32 + 192]
        mlo, mup = b * 64, (b + 5) * 64
        parts = [
            (kf[b * 128 : b * 128 + 384], vf[b * 128 : b * 128 + 384], 0.0, None),
            (km[mlo : mlo + 128], vm[mlo : mlo + 128], 1.0, None),
            (km[mup : mup + 128], vm[mup : mup + 128], 1.0, None),
            (kfar[...], vfar[...], 2.0, None),
            (kc[...], vc[...], 6.0, mask[b * 16 : b * 16 + 1, :]),
        ]
        all_scores = [scores(q, key) for key, _, _, _ in parts]
        tops = [
            jnp.max(s, axis=1, keepdims=True) * SCALE + size
            for s, (_, _, size, _) in zip(all_scores, parts)
        ]
        top = functools.reduce(jnp.maximum, tops)
        total = jnp.zeros((BLOCK, 2 * D), F32)
        for s, (_, value, size, keep) in zip(all_scores, parts):
            weights = jnp.exp2(s * SCALE - (top - size)).astype(BF)
            if keep is not None:
                weights = weights * keep
            total = total + jnp.dot(weights, value, preferred_element_type=F32)
        results.append((total[:, 0:D] / total[:, D : 2 * D]).astype(BF))
    out_first = jnp.concatenate(results[0:2], axis=0)
    out_second = jnp.concatenate(results[2:4], axis=0)
    own_out[...] = jnp.where(low, out_first, out_second)
    send_out[...] = jnp.where(low, out_second, out_first)


def attend(arrays):
    rows, cols = arrays[0].shape

    def spec(a):
        lead = a.shape[:-1]
        return pl.BlockSpec(lead + (D,), lambda h, n=len(lead): (0,) * n + (h,))

    coarse_n = 4 * arrays[-1].shape[1]
    out = jax.ShapeDtypeStruct((rows, cols), BF)
    return pl.pallas_call(
        attend_kernel,
        grid=(cols // D,),
        in_specs=[spec(a) for a in arrays],
        out_specs=[spec(out), spec(out)],
        out_shape=[out, out],
        scratch_shapes=[
            pltpu.VMEM((768, D), BF), pltpu.VMEM((768, 2 * D), BF),
            pltpu.VMEM((640, D), BF), pltpu.VMEM((640, 2 * D), BF),
            pltpu.VMEM((704, D), BF), pltpu.VMEM((704, 2 * D), BF),
            pltpu.VMEM((coarse_n, D), BF), pltpu.VMEM((coarse_n, 2 * D), BF),
            pltpu.VMEM((384, D), BF), pltpu.VMEM((384, 2 * D), BF),
            pltpu.VMEM((64, coarse_n), BF),
        ],
        compiler_params=pltpu.CompilerParams(vmem_limit_bytes=58 * 2**20),
        cost_estimate=pl.CostEstimate(
            flops=cols // D * 512 * 1536 * 2 * 384, bytes_accessed=16 * 2**20, transcendentals=cols // D * 512 * 1536
        ),
    )(*arrays)


def moved(a, axis, step):
    n = lax.axis_size(axis)
    return lax.ppermute(a, axis, [(i, (i + step) % n) for i in range(n)])


def shifted(a, step):
    n = lax.axis_size(YZ)
    return lax.ppermute(a, YZ, [(i, i + step) for i in range(n) if 0 <= i + step < n])


def per_device(queries, key_rows, value_rows):
    xl = lax.axis_index("xl")
    low = xl == 0
    half = queries.shape[1] // 2

    def mine(a):
        return lax.dynamic_slice_in_dim(a, xl * half, half, a.ndim - 1)

    def theirs(a):
        return lax.dynamic_slice_in_dim(a, (1 - xl) * half, half, a.ndim - 1)

    def swapped(a):
        return moved(a, "xl", 1)

    kv_send = jnp.stack([theirs(key_rows), theirs(value_rows)])
    kv_got = swapped(kv_send)
    kv_own = jnp.stack([mine(key_rows), mine(value_rows)])
    gathered = lax.all_gather(coarse_rows(kv_own, kv_send)[:, 0:8], Z)
    nz = gathered.shape[0]
    to_send = gathered[:, :, 4:8].reshape(nz * 8, half)
    q_send = theirs(queries)
    got = swapped(jnp.concatenate([q_send, to_send], axis=0))
    q_got = got[0 : q_send.shape[0]]
    coarse_got = got[q_send.shape[0] :].reshape(nz, 2, 4, half)
    coarse_own = gathered[:, :, 0:4]
    units = jnp.concatenate(
        [jnp.where(low, coarse_own, coarse_got), jnp.where(low, coarse_got, coarse_own)], axis=2
    )
    units = jnp.moveaxis(units, 1, 0).reshape(2, -1, half)
    coarse = (units, moved(units, "y", 1), moved(units, "y", -1), moved(units, "y", 2))
    q_own = mine(queries)
    kv_got, _ = lax.optimization_barrier((kv_got, gathered))
    up1, down1, mid, far = pooled(kv_own, kv_got)
    below1, above1 = shifted(up1, 1), shifted(down1, -1)
    below3, above3 = shifted(far[:, 96:128], 3), shifted(far[:, 0:32], -3)
    up, down, near = forwarded(below1, above1)
    below2, above2 = shifted(up, 1), shifted(down, -1)
    own_out, send_out = attend((
        q_own, q_got, kv_own, kv_got, mid, far, below1, above1, up, down, near, below2, above2, below3, above3,
        *coarse,
    ))
    got_out = swapped(send_out)
    return jnp.where(
        low,
        jnp.concatenate([own_out, got_out], axis=1),
        jnp.concatenate([got_out, own_out], axis=1),
    )


def solution(mesh):
    torus = Mesh(
        mesh.devices.reshape(4, 16, 2, mesh.shape["head"]), ("y", "z", "xl", "head")
    )
    spec = P(SEQ, "head")
    return jax.shard_map(
        per_device, mesh=torus, in_specs=(spec, spec, spec), out_specs=spec, check_vma=False
    )
```

```python
import functools
import math

import jax
import jax.numpy as jnp
from jax import lax
from jax.experimental import pallas as pl
from jax.experimental.pallas import tpu as pltpu
from jax.sharding import Mesh
from jax.sharding import PartitionSpec as P

D = 128
BLOCK = 128
FAR_REACH = 9
SEQ = ("y", "z", "xl")
YZ = ("y", "z")
Z = "z"
BF = jnp.bfloat16
F32 = jnp.float32
SCALE = math.log2(math.e) / math.sqrt(D)
VMEM = pltpu.CompilerParams(vmem_limit_bytes=58 * 2**20)


def taking(microseconds):
    return pl.CostEstimate(flops=0, bytes_accessed=int(microseconds * 3.6e6), transcendentals=0)


def halved(x, scratch):
    rows, cols = x.shape
    parts = []
    for c in range(cols // D):
        scratch[c, 0:rows] = x[:, c * D : (c + 1) * D]
        even = scratch[c, pl.ds(0, rows // 2, stride=2)]
        odd = scratch[c, pl.ds(1, rows // 2, stride=2)]
        parts.append((0.5 * (even + odd)).astype(BF))
    return parts[0] if len(parts) == 1 else jnp.concatenate(parts, axis=1)


def column(width, other=False):
    n = 8 * D // width

    def index(i, xl):
        return (0, (1 - xl[0] if other else xl[0]) * n + i)

    return index


def native_kernel(xl, k_own, k_send, v_own, v_send, unit_ref, far_ref, scratch):
    pieces = []
    for i, refs in enumerate(((k_own, k_send), (v_own, v_send))):
        for j, ref in enumerate(refs):
            four = halved(halved(ref[...].astype(F32), scratch).astype(F32), scratch)
            far_ref[j, i] = four
            rows, cols = four.shape
            pieces.append(jnp.sum(four.astype(F32).reshape(rows // 16, 16, cols), axis=1) * (1.0 / 16))
    unit_ref[...] = jnp.concatenate(pieces, axis=0).astype(BF)


def native_rows(xl, k, v):
    rows, cols = k.shape[0], k.shape[1] // 2
    width = 512
    own, send = (pl.BlockSpec((rows, width), column(width, other)) for other in (False, True))
    return pl.pallas_call(
        native_kernel,
        grid_spec=pltpu.PrefetchScalarGridSpec(
            num_scalar_prefetch=1,
            grid=(cols // width,),
            in_specs=[own, send, own, send],
            out_specs=[
                pl.BlockSpec((16, width), lambda c, xl: (0, c)),
                pl.BlockSpec((2, 2, rows // 4, width), lambda c, xl: (0, 0, 0, c)),
            ],
            scratch_shapes=[pltpu.VMEM((width // D, rows, D), F32)],
        ),
        out_shape=[jax.ShapeDtypeStruct((16, cols), BF), jax.ShapeDtypeStruct((2, 2, rows // 4, cols), BF)],
        compiler_params=VMEM,
        cost_estimate=taking(4),
    )(xl, k, k, v, v)


def pool_kernel(xl, k_ref, v_ref, got_ref, up_ref, down_ref, mid_ref, far_ref, scratch):
    low = xl[0] == 0
    for i, ref in enumerate((k_ref, v_ref)):
        own, got = ref[...], got_ref[i]
        first = jnp.where(low, own, got)
        second = jnp.where(low, got, own)
        mid_first = halved(first.astype(F32), scratch)
        mid_second = halved(second.astype(F32), scratch)
        far_first = halved(mid_first.astype(F32), scratch)
        far_second = halved(mid_second.astype(F32), scratch)
        mid_ref[i, 0:128] = mid_first
        mid_ref[i, 128:256] = mid_second
        far_ref[i, 0:64] = far_first
        far_ref[i, 64:128] = far_second
        up_ref[i, 0:128] = second[128:256]
        up_ref[i, 128:192] = mid_first[64:128]
        up_ref[i, 192:256] = mid_second[0:64]
        up_ref[i, 256:288] = far_first[0:32]
        down_ref[i, 0:128] = first[0:128]
        down_ref[i, 128:192] = mid_first[64:128]
        down_ref[i, 192:256] = mid_second[0:64]
        down_ref[i, 256:288] = far_second[32:64]


def pooled(xl, k, v, got):
    _, rows, cols = got.shape
    width = 256
    sizes = (288, 288, 256, 128)
    own = pl.BlockSpec((rows, width), column(width))
    return pl.pallas_call(
        pool_kernel,
        grid_spec=pltpu.PrefetchScalarGridSpec(
            num_scalar_prefetch=1,
            grid=(cols // width,),
            in_specs=[own, own, pl.BlockSpec((2, rows, width), lambda c, xl: (0, 0, c))],
            out_specs=[pl.BlockSpec((2, n, width), lambda c, xl: (0, 0, c)) for n in sizes],
            scratch_shapes=[pltpu.VMEM((width // D, rows, D), F32)],
        ),
        out_shape=[jax.ShapeDtypeStruct((2, n, cols), BF) for n in sizes],
        compiler_params=VMEM, cost_estimate=taking(5),
    )(xl, k, v, got)


def flags(blocks, first, unit, ref):
    ny, nz = lax.axis_size("y"), lax.axis_size("z")
    at = 4 * (lax.axis_index("y") * nz + lax.axis_index("z"))
    block = first + lax.broadcasted_iota(jnp.int32, (blocks * unit, D), 0) // unit + at
    ref[:, D : 2 * D] = jnp.where((block >= 0) & (block < 4 * ny * nz), 1.0, 0.0).astype(BF)


def present():
    ny, nz = lax.axis_size("y"), lax.axis_size("z")
    zz = lax.axis_index("y") * nz + lax.axis_index("z")
    return [zz >= n for n in range(4)], [zz <= ny * nz - 1 - n for n in range(4)]


def put(ref, start, rows, here, fallback):
    ref[start : start + rows.shape[0], 0:D] = rows if fallback is None else jnp.where(here, rows, fallback)


def scores(q, key):
    return lax.dot_general(q, key, (((1,), (1,)), ((), ())), preferred_element_type=F32)


def weighted(parts, top):
    total = jnp.zeros((BLOCK, 2 * D), F32)
    for s, value, size, keep in parts:
        weights = jnp.exp2(s * SCALE - (top - size)).astype(BF)
        if keep is not None:
            weights = weights * keep
        total = total + jnp.dot(weights, value, preferred_element_type=F32)
    return total


def top_of(parts):
    return functools.reduce(
        jnp.maximum, [jnp.max(s, axis=1, keepdims=True) * SCALE + size for s, _, size, _ in parts]
    )


def near_kernel(
    xl, q_own, q_got, k_own, v_own, kv_got, mid, far, below1, above1,
    below_own, below_got, above_own, above_got, edge_own, edge_got,
    out, stat, kf, vf, km, vm, kr, vr, kfar, vfar, scratch,
):
    low = xl[0] == 0

    @pl.when(pl.program_id(0) == 0)
    def _():
        flags(6, -1, 128, vf)
        flags(10, -3, 64, vm)
        flags(22, -9, 32, vr)

    has, has_up = present()
    for i, (own_ref, fine_w, mid_w, far_w) in enumerate(((k_own, kf, km, kr), (v_own, vf, vm, vr))):
        is_key = i == 0

        def spare(rows):
            return rows if is_key else None

        own, got = own_ref[...], kv_got[i]
        first, second = jnp.where(low, own, got), jnp.where(low, got, own)
        fine_w[128:384, 0:D] = first
        fine_w[384:640, 0:D] = second
        put(fine_w, 0, below1[i, 0:128], has[1], spare(first[0:128]))
        put(fine_w, 640, above1[i, 0:128], has_up[1], spare(second[128:256]))
        mid_w[192:448, 0:D] = mid[i]
        m0, m3 = spare(mid[i, 0:64]), spare(mid[i, 192:256])
        mid_below = halved(below1[i, 0:128].astype(F32), scratch)
        mid_above = halved(above1[i, 0:128].astype(F32), scratch)
        put(mid_w, 0, below1[i, 128:192], has[1], m0)
        put(mid_w, 64, below1[i, 192:256], has[1], m0)
        put(mid_w, 128, mid_below, has[1], m0)
        put(mid_w, 448, mid_above, has_up[1], m3)
        put(mid_w, 512, above1[i, 128:192], has_up[1], m3)
        put(mid_w, 576, above1[i, 192:256], has_up[1], m3)
        far_w[288:416, 0:D] = far[i]
        f0, f3 = far[i, 0:32], far[i, 96:128]
        f0_2, f3_2 = spare(jnp.concatenate([f0] * 2, axis=0)), spare(jnp.concatenate([f3] * 2, axis=0))
        f0_3, f3_3 = spare(jnp.concatenate([f0] * 3, axis=0)), spare(jnp.concatenate([f3] * 3, axis=0))
        put(far_w, 0, jnp.where(low, edge_got[i], edge_own[i]), has[3], spare(f0))
        put(far_w, 32, jnp.where(low, below_own[i], below_got[i]), has[2], f0_2)
        put(far_w, 96, jnp.where(low, below_got[i], below_own[i]), has[2], f0_2)
        put(far_w, 160, below1[i, 256:288], has[1], spare(f0))
        rows = jnp.concatenate([below1[i, 128:256], mid_below], axis=0)
        put(far_w, 192, halved(rows.astype(F32), scratch), has[1], f0_3)
        rows = jnp.concatenate([mid_above, above1[i, 128:256]], axis=0)
        put(far_w, 416, halved(rows.astype(F32), scratch), has_up[1], f3_3)
        put(far_w, 512, above1[i, 256:288], has_up[1], spare(f3))
        put(far_w, 544, jnp.where(low, above_own[i], above_got[i]), has_up[2], f3_2)
        put(far_w, 608, jnp.where(low, above_got[i], above_own[i]), has_up[2], f3_2)
        put(far_w, 672, jnp.where(low, edge_own[i], edge_got[i]), has_up[3], spare(f3))
    qo, qg = q_own[...], q_got[...]
    queries = (jnp.where(low, qo, qg), jnp.where(low, qg, qo))
    left = lax.broadcasted_iota(jnp.int32, (BLOCK, D), 1) < D // 2
    for b in range(4):
        q = queries[b // 2][(b % 2) * 128 : (b % 2 + 1) * 128]
        kfar[0:192] = kr[b * 32 : b * 32 + 192]
        kfar[192:384] = kr[(b + 13) * 32 : (b + 13) * 32 + 192]
        vfar[0:192] = vr[b * 32 : b * 32 + 192]
        vfar[192:384] = vr[(b + 13) * 32 : (b + 13) * 32 + 192]
        lo, up = b * 64, (b + 5) * 64
        parts = [
            (scores(q, kf[b * 128 : b * 128 + 384]), vf[b * 128 : b * 128 + 384], 0.0, None),
            (scores(q, km[lo : lo + 128]), vm[lo : lo + 128], 1.0, None),
            (scores(q, km[up : up + 128]), vm[up : up + 128], 1.0, None),
            (scores(q, kfar[...]), vfar[...], 2.0, None),
        ]
        top = top_of(parts)
        total = weighted(parts, top)
        out[b * 128 : (b + 1) * 128] = total[:, 0:D]
        stat[b * 128 : (b + 1) * 128] = jnp.where(left, top, total[:, D : 2 * D])


def far_kernel(xl, q_own, q_got, coarse, near_out, near_stat, own_out, send_out, kc, vc, mask):
    low = xl[0] == 0
    y = lax.axis_index("y")
    ny, nz = lax.axis_size("y"), lax.axis_size("z")
    coarse_n = coarse.shape[0] * coarse.shape[2]

    @pl.when(pl.program_id(0) == 0)
    def _():
        vc[:, D : 2 * D] = jnp.ones((coarse_n, D), BF)
        at = lax.broadcasted_iota(jnp.int32, (16, coarse_n), 1)
        turn = (at // 8) % ny
        other = (y + jnp.where(turn == 0, 0, jnp.where(turn == 1, ny - 1, jnp.where(turn == 2, 1, 2)))) % ny
        block = (other * nz + at // (8 * ny)) * 4 + (at % 8) // 2
        for b in range(4):
            gap = jnp.abs(block - (4 * (y * nz + lax.axis_index("z")) + b))
            mask[b * 16 : (b + 1) * 16, :] = jnp.where(gap > FAR_REACH, 1.0, 0.0).astype(BF)

    kc[...] = coarse[:, 0].reshape(coarse_n, D)
    vc[:, 0:D] = coarse[:, 1].reshape(coarse_n, D)
    qo, qg = q_own[...], q_got[...]
    queries = (jnp.where(low, qo, qg), jnp.where(low, qg, qo))
    results = []
    for b in range(4):
        q = queries[b // 2][(b % 2) * 128 : (b % 2 + 1) * 128]
        parts = [(scores(q, kc[...]), vc[...], 6.0, mask[b * 16 : b * 16 + 1, :])]
        here = slice(b * 128, (b + 1) * 128)
        near_top, near_sum = near_stat[here, 0:1], near_stat[here, D - 1 : D]
        top = jnp.maximum(top_of(parts), near_top)
        total = weighted(parts, top)
        scale = jnp.exp2(near_top - top)
        upper = total[:, 0:D] + near_out[here] * scale
        results.append((upper / (total[:, D : 2 * D] + near_sum * scale)).astype(BF))
    out_first = jnp.concatenate(results[0:2], axis=0)
    out_second = jnp.concatenate(results[2:4], axis=0)
    own_out[...] = jnp.where(low, out_first, out_second)
    send_out[...] = jnp.where(low, out_second, out_first)


def by_head(a):
    lead = a.shape[:-1]
    return pl.BlockSpec(lead + (D,), lambda h, xl, n=len(lead): (0,) * n + (h,))


def attend_call(kernel, xl, own, arrays, outs, out_specs, scratch, cost):
    rows, cols = own[0].shape[0], own[0].shape[1] // 2
    spec_own = pl.BlockSpec((rows, D), column(D))
    order = [(own[0], spec_own), (arrays[0], by_head(arrays[0]))]
    order += [(a, spec_own) for a in own[1:]] + [(a, by_head(a)) for a in arrays[1:]]
    return pl.pallas_call(
        kernel,
        grid_spec=pltpu.PrefetchScalarGridSpec(
            num_scalar_prefetch=1,
            grid=(cols // D,),
            in_specs=[spec for _, spec in order],
            out_specs=out_specs,
            scratch_shapes=scratch,
        ),
        out_shape=outs,
        compiler_params=VMEM,
        cost_estimate=taking(cost),
    )(xl, *(a for a, _ in order))


def attend_near(xl, q, q_got, k, v, arrays):
    rows, cols = q.shape[0], q.shape[1] // 2
    outs = [jax.ShapeDtypeStruct((2 * rows, cols), F32)] * 2
    scratch = [
        pltpu.VMEM((768, D), BF), pltpu.VMEM((768, 2 * D), BF),
        pltpu.VMEM((640, D), BF), pltpu.VMEM((640, 2 * D), BF),
        pltpu.VMEM((704, D), BF), pltpu.VMEM((704, 2 * D), BF),
        pltpu.VMEM((384, D), BF), pltpu.VMEM((384, 2 * D), BF),
        pltpu.VMEM((1, 192, D), F32),
    ]
    return attend_call(
        near_kernel, xl, (q, k, v), (q_got, *arrays), outs, [by_head(a) for a in outs], scratch, 15
    )


def attend_far(xl, q, q_got, arrays):
    rows, cols = q.shape[0], q.shape[1] // 2
    outs = [jax.ShapeDtypeStruct((rows, 2 * cols), BF), jax.ShapeDtypeStruct((rows, cols), BF)]
    coarse_n = arrays[0].shape[0] * arrays[0].shape[2]
    scratch = [
        pltpu.VMEM((coarse_n, D), BF), pltpu.VMEM((coarse_n, 2 * D), BF),
        pltpu.VMEM((64, coarse_n), BF),
    ]
    return attend_call(
        far_kernel, xl, (q,), (q_got, *arrays), outs,
        [pl.BlockSpec((rows, D), column(D)), by_head(outs[1])], scratch, 9,
    )


def moved(a, axis, step):
    n = lax.axis_size(axis)
    return lax.ppermute(a, axis, [(i, (i + step) % n) for i in range(n)])


def shifted(a, step):
    n = lax.axis_size(YZ)
    return lax.ppermute(a, YZ, [(i, i + step) for i in range(n) if 0 <= i + step < n])


def outward(a):
    n = lax.axis_size(YZ)
    route = [(2 * i, 2 * i - 2) for i in range(1, n)] + [(2 * i + 1, 2 * i + 3) for i in range(n - 1)]
    return lax.ppermute(a, SEQ, route)


def per_device(queries, key_rows, value_rows):
    xl = lax.axis_index("xl")
    low = xl == 0
    at = xl.reshape(1)
    half = queries.shape[1] // 2

    def theirs(a):
        return lax.dynamic_slice_in_dim(a, (1 - xl) * half, half, a.ndim - 1)

    def swapped(a):
        return moved(a, "xl", 1)

    kv_send, keys, values = lax.optimization_barrier(
        (jnp.stack([theirs(key_rows), theirs(value_rows)]), key_rows, value_rows)
    )
    kv_got = swapped(kv_send)
    unit, fours = native_rows(at, keys, values)
    turned = (moved(unit, "y", 1), moved(unit, "y", -1), moved(unit, "y", 2))
    below2, above2 = shifted(fours, 2), shifted(fours, -2)
    units = jnp.concatenate([unit, *turned], axis=0)
    units_got = swapped(units)
    kept = units.reshape(4, 2, 8, half)[:, :, 0:4]
    came = units_got.reshape(4, 2, 8, half)[:, :, 4:8]
    units = jnp.concatenate([jnp.where(low, kept, came), jnp.where(low, came, kept)], axis=2)
    units = jnp.moveaxis(units, 1, 0).reshape(2, 32, half)
    units, _, _, _ = lax.optimization_barrier((units, kv_got, below2, above2))
    coarse = lax.all_gather(units, "z")
    edge = outward(jnp.where(low, above2[:, :, 0:32], below2[:, :, 32:64]))
    sent = (theirs(queries), below2[1], above2[1], edge[1])
    up1, down1, mid, far = pooled(at, key_rows, value_rows, kv_got)
    message = jnp.concatenate([a.reshape(-1, half) for a in sent], axis=0)
    message, up1, down1 = lax.optimization_barrier((message, up1, down1))
    got = swapped(message)
    q_got, below_got, above_got, edge_got = (
        got[i:j].reshape(a.shape) for a, i, j in zip(sent, (0, 256, 384, 512), (256, 384, 512, 576))
    )
    below1, above1 = shifted(up1, 1), shifted(down1, -1)
    near_out, near_stat = attend_near(
        at, queries, q_got, key_rows, value_rows,
        (kv_got, mid, far, below1, above1, below2[0], below_got, above2[0], above_got, edge[0], edge_got),
    )
    out, send_out = attend_far(at, queries, q_got, (coarse, near_out, near_stat))
    return lax.dynamic_update_slice_in_dim(out, swapped(send_out), (1 - xl) * half, 1)


def solution(mesh):
    torus = Mesh(
        mesh.devices.reshape(4, 16, 2, mesh.shape["head"]), ("y", "z", "xl", "head")
    )
    spec = P(SEQ, "head")
    return jax.shard_map(
        per_device, mesh=torus, in_specs=(spec, spec, spec), out_specs=spec, check_vma=False
    )
```

```python
import functools
import math

import jax
import jax.numpy as jnp
from jax import lax
from jax.experimental import pallas as pl
from jax.experimental.pallas import tpu as pltpu
from jax.sharding import Mesh
from jax.sharding import PartitionSpec as P

D = 128
BLOCK = 128
FAR_REACH = 9
LOWEST = 7
SEQ = ("y", "z", "xl")
YZ = ("y", "z")
Z = "z"
BF = jnp.bfloat16
F32 = jnp.float32
SCALE = math.log2(math.e) / math.sqrt(D)
VMEM = pltpu.CompilerParams(vmem_limit_bytes=58 * 2**20)


def taking(microseconds):
    return pl.CostEstimate(flops=0, bytes_accessed=int(microseconds * 3.6e6), transcendentals=0)


def halved(x, scratch):
    rows, cols = x.shape
    parts = []
    for c in range(cols // D):
        scratch[c, 0:rows] = x[:, c * D : (c + 1) * D]
        even = scratch[c, pl.ds(0, rows // 2, stride=2)]
        odd = scratch[c, pl.ds(1, rows // 2, stride=2)]
        parts.append((0.5 * (even + odd)).astype(BF))
    return parts[0] if len(parts) == 1 else jnp.concatenate(parts, axis=1)


def column(width, other=False):
    n = 8 * D // width

    def index(i, xl):
        return (0, (1 - xl[0] if other else xl[0]) * n + i)

    return index


def native_kernel(xl, k_own, k_send, v_own, v_send, unit_ref, far_ref, scratch):
    pieces = []
    for i, refs in enumerate(((k_own, k_send), (v_own, v_send))):
        for j, ref in enumerate(refs):
            four = halved(halved(ref[...].astype(F32), scratch).astype(F32), scratch)
            far_ref[j, i] = jnp.where(xl[0] == 0, four[0:32], four[32:64])
            rows, cols = four.shape
            pieces.append(jnp.sum(four.astype(F32).reshape(rows // 16, 16, cols), axis=1) * (1.0 / 16))
    unit_ref[...] = jnp.concatenate(pieces, axis=0).astype(BF)


def native_rows(xl, k, v):
    rows, cols = k.shape[0], k.shape[1] // 2
    width = 512
    own, send = (pl.BlockSpec((rows, width), column(width, other)) for other in (False, True))
    return pl.pallas_call(
        native_kernel,
        grid_spec=pltpu.PrefetchScalarGridSpec(
            num_scalar_prefetch=1,
            grid=(cols // width,),
            in_specs=[own, send, own, send],
            out_specs=[
                pl.BlockSpec((16, width), lambda c, xl: (0, c)),
                pl.BlockSpec((2, 2, rows // 8, width), lambda c, xl: (0, 0, 0, c)),
            ],
            scratch_shapes=[pltpu.VMEM((width // D, rows, D), F32)],
        ),
        out_shape=[jax.ShapeDtypeStruct((16, cols), BF), jax.ShapeDtypeStruct((2, 2, rows // 8, cols), BF)],
        compiler_params=VMEM,
        cost_estimate=taking(4),
    )(xl, k, k, v, v)


def arrange_kernel(*refs):
    *parts, out_ref = refs
    rows = jnp.concatenate([ref[...].astype(F32) for ref in parts], axis=0)
    n, cols = rows.shape
    rows = rows.reshape(n // 16, 2, 8, cols)
    for i in range(2):
        out_ref[i] = rows[:, i].reshape(n // 2, cols).astype(BF)


def arranged(*parts):
    n, cols = sum(a.shape[0] for a in parts), parts[0].shape[1]
    width = 256
    return pl.pallas_call(
        arrange_kernel,
        grid=(cols // width,),
        in_specs=[pl.BlockSpec((a.shape[0], width), lambda c: (0, c)) for a in parts],
        out_specs=pl.BlockSpec((2, n // 2, width), lambda c: (0, 0, c)),
        out_shape=jax.ShapeDtypeStruct((2, n // 2, cols), BF),
        compiler_params=VMEM,
        cost_estimate=taking(2),
    )(*parts)


def pool_kernel(xl, k_ref, v_ref, got_ref, up_ref, down_ref, mid_ref, far_ref, scratch):
    low = xl[0] == 0
    for i, ref in enumerate((k_ref, v_ref)):
        own, got = ref[...], got_ref[i]
        first = jnp.where(low, own, got)
        second = jnp.where(low, got, own)
        mid_first = halved(first.astype(F32), scratch)
        mid_second = halved(second.astype(F32), scratch)
        far_first = halved(mid_first.astype(F32), scratch)
        far_second = halved(mid_second.astype(F32), scratch)
        mid_ref[i, 0:128] = mid_first
        mid_ref[i, 128:256] = mid_second
        far_ref[i, 0:64] = far_first
        far_ref[i, 64:128] = far_second
        up_ref[i, 0:128] = second[128:256]
        up_ref[i, 128:192] = mid_first[64:128]
        up_ref[i, 192:256] = mid_second[0:64]
        up_ref[i, 256:288] = far_first[0:32]
        down_ref[i, 0:128] = first[0:128]
        down_ref[i, 128:192] = mid_first[64:128]
        down_ref[i, 192:256] = mid_second[0:64]
        down_ref[i, 256:288] = far_second[32:64]


def pooled(xl, k, v, got):
    _, rows, cols = got.shape
    width = 256
    sizes = (288, 288, 256, 128)
    own = pl.BlockSpec((rows, width), column(width))
    return pl.pallas_call(
        pool_kernel,
        grid_spec=pltpu.PrefetchScalarGridSpec(
            num_scalar_prefetch=1,
            grid=(cols // width,),
            in_specs=[own, own, pl.BlockSpec((2, rows, width), lambda c, xl: (0, 0, c))],
            out_specs=[pl.BlockSpec((2, n, width), lambda c, xl: (0, 0, c)) for n in sizes],
            scratch_shapes=[pltpu.VMEM((width // D, rows, D), F32)],
        ),
        out_shape=[jax.ShapeDtypeStruct((2, n, cols), BF) for n in sizes],
        compiler_params=VMEM, cost_estimate=taking(5),
    )(xl, k, v, got)


def forward_kernel(below_ref, above_ref, up_ref, down_ref, near_ref, scratch):
    below, above = below_ref[0], above_ref[0]
    below_near = halved(below[0:128].astype(F32), scratch)
    above_near = halved(above[0:128].astype(F32), scratch)
    near_ref[0, 0:64] = below_near
    near_ref[0, 64:128] = above_near
    up_ref[0, 0:32] = below[256:288]
    up_ref[0, 32:128] = halved(jnp.concatenate([below[128:256], below_near], axis=0).astype(F32), scratch)
    down_ref[0, 0:96] = halved(jnp.concatenate([above_near, above[128:256]], axis=0).astype(F32), scratch)
    down_ref[0, 96:128] = above[256:288]


def forwarded(below, above):
    _, rows, cols = below.shape
    width = 512
    return pl.pallas_call(
        forward_kernel,
        grid=(2, cols // width),
        in_specs=[pl.BlockSpec((1, rows, width), lambda i, c: (i, 0, c))] * 2,
        out_specs=[pl.BlockSpec((1, 128, width), lambda i, c: (i, 0, c))] * 3,
        out_shape=[jax.ShapeDtypeStruct((2, 128, cols), BF)] * 3,
        scratch_shapes=[pltpu.VMEM((width // D, 192, D), F32)],
        compiler_params=VMEM, cost_estimate=taking(4),
    )(below, above)


def flags(blocks, first, unit, ref):
    ny, nz = lax.axis_size("y"), lax.axis_size("z")
    at = 4 * (lax.axis_index("y") * nz + lax.axis_index("z"))
    block = first + lax.broadcasted_iota(jnp.int32, (blocks * unit, D), 0) // unit + at
    ref[:, D : 2 * D] = jnp.where((block >= 0) & (block < 4 * ny * nz), 1.0, 0.0).astype(BF)


def present():
    ny, nz = lax.axis_size("y"), lax.axis_size("z")
    zz = lax.axis_index("y") * nz + lax.axis_index("z")
    return [zz >= n for n in range(4)], [zz <= ny * nz - 1 - n for n in range(4)]


def put(ref, start, rows, here, fallback):
    ref[start : start + rows.shape[0], 0:D] = rows if fallback is None else jnp.where(here, rows, fallback)


def scores(q, key):
    return lax.dot_general(q, key, (((1,), (1,)), ((), ())), preferred_element_type=F32)


def weighted(parts, top):
    total = jnp.zeros((BLOCK, 2 * D), F32)
    for s, value, size, keep in parts:
        weights = jnp.exp2(s * SCALE - (top - size)).astype(BF)
        if keep is not None:
            weights = weights * keep
        total = total + jnp.dot(weights, value, preferred_element_type=F32)
    return total


def top_of(parts):
    return functools.reduce(
        jnp.maximum, [jnp.max(s, axis=1, keepdims=True) * SCALE + size for s, _, size, _ in parts]
    )


def near_kernel(
    xl, q_own, q_got, k_own, v_own, kv_got, mid, below1, above1, near, coarse0, coarse1, coarse2, coarse3,
    out, stat, kf, vf, km, vm, kc, vc, mask,
):
    low = xl[0] == 0
    coarse_n = mask.shape[1]

    @pl.when(pl.program_id(0) == 0)
    def _():
        flags(6, -1, 128, vf)
        flags(10, -3, 64, vm)
        vc[:, D : 2 * D] = jnp.ones((coarse_n, D), BF)
        y, z = lax.axis_index("y"), lax.axis_index("z")
        ny, nz = lax.axis_size("y"), lax.axis_size("z")
        at = lax.broadcasted_iota(jnp.int32, (16, coarse_n), 1)
        turn = at // (8 * nz)
        other_y = (y + jnp.where(turn == 0, 0, jnp.where(turn == 1, ny - 1, jnp.where(turn == 2, 1, 2)))) % ny
        other_z = (z + (at // 8) % nz + nz - LOWEST) % nz
        block = (other_y * nz + other_z) * 4 + (at % 8) // 2
        for b in range(4):
            gap = jnp.abs(block - (4 * (y * nz + z) + b))
            mask[b * 16 : (b + 1) * 16, :] = jnp.where(gap > FAR_REACH, 1.0, 0.0).astype(BF)

    has, has_up = present()
    for i, (own_ref, fine_w, mid_w) in enumerate(((k_own, kf, km), (v_own, vf, vm))):
        is_key = i == 0
        own, got = own_ref[...], kv_got[i]
        first, second = jnp.where(low, own, got), jnp.where(low, got, own)
        fine_w[128:384, 0:D] = first
        fine_w[384:640, 0:D] = second
        put(fine_w, 0, below1[i, 0:128], has[1], first[0:128] if is_key else None)
        put(fine_w, 640, above1[i, 0:128], has_up[1], second[128:256] if is_key else None)
        mid_w[192:448, 0:D] = mid[i]
        m0 = mid[i, 0:64] if is_key else None
        m3 = mid[i, 192:256] if is_key else None
        put(mid_w, 0, below1[i, 128:192], has[1], m0)
        put(mid_w, 64, below1[i, 192:256], has[1], m0)
        put(mid_w, 128, near[i, 0:64], has[1], m0)
        put(mid_w, 448, near[i, 64:128], has_up[1], m3)
        put(mid_w, 512, above1[i, 128:192], has_up[1], m3)
        put(mid_w, 576, above1[i, 192:256], has_up[1], m3)
    step = coarse_n // 4
    for t, part in enumerate((coarse0, coarse1, coarse2, coarse3)):
        kc[t * step : (t + 1) * step] = part[0]
        vc[t * step : (t + 1) * step, 0:D] = part[1]
    qo, qg = q_own[...], q_got[...]
    queries = (jnp.where(low, qo, qg), jnp.where(low, qg, qo))
    left = lax.broadcasted_iota(jnp.int32, (BLOCK, D), 1) < D // 2
    for b in range(4):
        q = queries[b // 2][(b % 2) * 128 : (b % 2 + 1) * 128]
        lo, up = b * 64, (b + 5) * 64
        parts = [
            (scores(q, kf[b * 128 : b * 128 + 384]), vf[b * 128 : b * 128 + 384], 0.0, None),
            (scores(q, km[lo : lo + 128]), vm[lo : lo + 128], 1.0, None),
            (scores(q, km[up : up + 128]), vm[up : up + 128], 1.0, None),
            (scores(q, kc[...]), vc[...], 6.0, mask[b * 16 : b * 16 + 1, :]),
        ]
        top = top_of(parts)
        total = weighted(parts, top)
        out[b * 128 : (b + 1) * 128] = total[:, 0:D]
        stat[b * 128 : (b + 1) * 128] = jnp.where(left, top, total[:, D : 2 * D])


def far_kernel(
    xl, q_own, q_got, far, up, down, below2, above2, edge_own, edge_got, near_out, near_stat,
    own_out, send_out, kr, vr, kfar, vfar,
):
    low = xl[0] == 0

    @pl.when(pl.program_id(0) == 0)
    def _():
        flags(22, -9, 32, vr)

    has, has_up = present()
    for i, far_w in enumerate((kr, vr)):
        is_key = i == 0
        far_w[288:416, 0:D] = far[i]
        f0 = far[i, 0:32] if is_key else None
        f3 = far[i, 96:128] if is_key else None
        f0_4 = jnp.concatenate([f0] * 4, axis=0) if is_key else None
        f3_4 = jnp.concatenate([f3] * 4, axis=0) if is_key else None
        put(far_w, 0, jnp.where(low, edge_got[i], edge_own[i]), has[3], f0)
        put(far_w, 32, below2[i], has[2], f0_4)
        put(far_w, 160, up[i], has[1], f0_4)
        put(far_w, 416, down[i], has_up[1], f3_4)
        put(far_w, 544, above2[i], has_up[2], f3_4)
        put(far_w, 672, jnp.where(low, edge_own[i], edge_got[i]), has_up[3], f3)
    qo, qg = q_own[...], q_got[...]
    queries = (jnp.where(low, qo, qg), jnp.where(low, qg, qo))
    results = []
    for b in range(4):
        q = queries[b // 2][(b % 2) * 128 : (b % 2 + 1) * 128]
        kfar[b, 0:192] = kr[b * 32 : b * 32 + 192]
        kfar[b, 192:384] = kr[(b + 13) * 32 : (b + 13) * 32 + 192]
        vfar[b, 0:192] = vr[b * 32 : b * 32 + 192]
        vfar[b, 192:384] = vr[(b + 13) * 32 : (b + 13) * 32 + 192]
        parts = [(scores(q, kfar[b]), vfar[b], 2.0, None)]
        here = slice(b * 128, (b + 1) * 128)
        near_top, near_sum = near_stat[here, 0:1], near_stat[here, D - 1 : D]
        top = jnp.maximum(top_of(parts), near_top)
        total = weighted(parts, top)
        scale = jnp.exp2(near_top - top)
        upper = total[:, 0:D] + near_out[here] * scale
        results.append((upper / (total[:, D : 2 * D] + near_sum * scale)).astype(BF))
    out_first = jnp.concatenate(results[0:2], axis=0)
    out_second = jnp.concatenate(results[2:4], axis=0)
    own_out[...] = jnp.where(low, out_first, out_second)
    send_out[...] = jnp.where(low, out_second, out_first)


def by_head(a):
    lead = a.shape[:-1]
    return pl.BlockSpec(lead + (D,), lambda h, xl, n=len(lead): (0,) * n + (h,))


def attend_call(kernel, xl, own, arrays, outs, out_specs, scratch, cost):
    rows, cols = own[0].shape[0], own[0].shape[1] // 2
    spec_own = pl.BlockSpec((rows, D), column(D))
    order = [(own[0], spec_own), (arrays[0], by_head(arrays[0]))]
    order += [(a, spec_own) for a in own[1:]] + [(a, by_head(a)) for a in arrays[1:]]
    return pl.pallas_call(
        kernel,
        grid_spec=pltpu.PrefetchScalarGridSpec(
            num_scalar_prefetch=1,
            grid=(cols // D,),
            in_specs=[spec for _, spec in order],
            out_specs=out_specs,
            scratch_shapes=scratch,
        ),
        out_shape=outs,
        compiler_params=VMEM,
        cost_estimate=taking(cost),
    )(xl, *(a for a, _ in order))


def attend_near(xl, q, q_got, k, v, arrays):
    rows, cols = q.shape[0], q.shape[1] // 2
    outs = [jax.ShapeDtypeStruct((2 * rows, cols), F32)] * 2
    coarse_n = 4 * arrays[-1].shape[1]
    scratch = [
        pltpu.VMEM((768, D), BF), pltpu.VMEM((768, 2 * D), BF),
        pltpu.VMEM((640, D), BF), pltpu.VMEM((640, 2 * D), BF),
        pltpu.VMEM((coarse_n, D), BF), pltpu.VMEM((coarse_n, 2 * D), BF),
        pltpu.VMEM((64, coarse_n), BF),
    ]
    return attend_call(
        near_kernel, xl, (q, k, v), (q_got, *arrays), outs, [by_head(a) for a in outs], scratch, 16
    )


def attend_far(xl, q, q_got, arrays):
    rows, cols = q.shape[0], q.shape[1] // 2
    outs = [jax.ShapeDtypeStruct((rows, 2 * cols), BF), jax.ShapeDtypeStruct((rows, cols), BF)]
    scratch = [
        pltpu.VMEM((704, D), BF), pltpu.VMEM((704, 2 * D), BF),
        pltpu.VMEM((4, 384, D), BF), pltpu.VMEM((4, 384, 2 * D), BF),
    ]
    return attend_call(
        far_kernel, xl, (q,), (q_got, *arrays), outs,
        [pl.BlockSpec((rows, D), column(D)), by_head(outs[1])], scratch, 9,
    )


def moved(a, axis, step):
    n = lax.axis_size(axis)
    return lax.ppermute(a, axis, [(i, (i + step) % n) for i in range(n)])


def shifted(a, step):
    n = lax.axis_size(YZ)
    return lax.ppermute(a, YZ, [(i, i + step) for i in range(n) if 0 <= i + step < n])


def outward(a, step):
    n = lax.axis_size(YZ)
    route = [(2 * i, 2 * (i - step)) for i in range(step, n)]
    route += [(2 * i + 1, 2 * (i + step) + 1) for i in range(n - step)]
    return lax.ppermute(a, SEQ, route)


def per_device(queries, key_rows, value_rows):
    xl = lax.axis_index("xl")
    low = xl == 0
    at = xl.reshape(1)
    half = queries.shape[1] // 2

    def theirs(a):
        return lax.dynamic_slice_in_dim(a, (1 - xl) * half, half, a.ndim - 1)

    def swapped(a):
        return moved(a, "xl", 1)

    kv_send, keys, values = lax.optimization_barrier(
        (jnp.stack([theirs(key_rows), theirs(value_rows)]), key_rows, value_rows)
    )
    kv_got = swapped(kv_send)
    unit, outer = native_rows(at, keys, values)
    unit_got = swapped(unit)
    kept = unit.reshape(2, 8, half)[:, 0:4]
    came = unit_got.reshape(2, 8, half)[:, 4:8]
    unit = jnp.concatenate([jnp.where(low, kept, came), jnp.where(low, came, kept)], axis=1).reshape(16, half)
    units = jnp.concatenate([moved(unit, "z", 1), unit, moved(unit, "z", -1)], axis=0)
    units = jnp.concatenate([moved(units, "z", 3), units, moved(units, "z", -3)], axis=0)
    lower, upper = units[16:64], units[80:144]
    lower, upper, _, outer = lax.optimization_barrier((lower, upper, kv_got, outer))
    units = arranged(moved(lower, "z", 4), units, moved(upper, "z", -4))
    up1, down1, mid, far = pooled(at, key_rows, value_rows, kv_got)
    up1, down1, units = lax.optimization_barrier((up1, down1, units))
    below1, above1 = shifted(up1, 1), shifted(down1, -1)
    coarse = (units, moved(units, "y", 1), moved(units, "y", -1), moved(units, "y", 2))
    edge = outward(outer, 3)
    message = jnp.concatenate([theirs(queries), edge[1].reshape(-1, half)], axis=0)
    got = swapped(message)
    q_got, edge_got = got[0 : queries.shape[0]], got[queries.shape[0] :].reshape(edge[1].shape)
    up, down, near = forwarded(below1, above1)
    below2, above2 = shifted(up, 1), shifted(down, -1)
    near_out, near_stat = attend_near(
        at, queries, q_got, key_rows, value_rows, (kv_got, mid, below1, above1, near, *coarse)
    )
    out, send_out = attend_far(
        at, queries, q_got, (far, up, down, below2, above2, edge[0], edge_got, near_out, near_stat)
    )
    return lax.dynamic_update_slice_in_dim(out, swapped(send_out), (1 - xl) * half, 1)


def solution(mesh):
    torus = Mesh(
        mesh.devices.reshape(4, 16, 2, mesh.shape["head"]), ("y", "z", "xl", "head")
    )
    spec = P(SEQ, "head")
    return jax.shard_map(
        per_device, mesh=torus, in_specs=(spec, spec, spec), out_specs=spec, check_vma=False
    )
```

```python
import functools
import math

import jax
import jax.numpy as jnp
from jax import lax
from jax.experimental import pallas as pl
from jax.experimental.pallas import tpu as pltpu
from jax.sharding import Mesh
from jax.sharding import PartitionSpec as P

D = 128
BLOCK = 128
FAR_REACH = 9
SEQ = ("y", "z", "xl")
YZ = ("y", "z")
Z = "z"
BF = jnp.bfloat16
F32 = jnp.float32
SCALE = math.log2(math.e) / math.sqrt(D)
VMEM = pltpu.CompilerParams(vmem_limit_bytes=58 * 2**20)


def taking(microseconds):
    return pl.CostEstimate(flops=0, bytes_accessed=int(microseconds * 3.6e6), transcendentals=0)


def halved(x, scratch):
    rows, cols = x.shape
    parts = []
    for c in range(cols // D):
        scratch[c, 0:rows] = x[:, c * D : (c + 1) * D]
        even = scratch[c, pl.ds(0, rows // 2, stride=2)]
        odd = scratch[c, pl.ds(1, rows // 2, stride=2)]
        parts.append((0.5 * (even + odd)).astype(BF))
    return parts[0] if len(parts) == 1 else jnp.concatenate(parts, axis=1)


def column(width, other=False):
    n = 8 * D // width

    def index(i, xl):
        return (0, (1 - xl[0] if other else xl[0]) * n + i)

    return index


def coarse_kernel(xl, k_own, k_send, v_own, v_send, unit_ref, scratch):
    pieces = []
    for ref in (k_own, k_send, v_own, v_send):
        four = halved(halved(ref[...].astype(F32), scratch).astype(F32), scratch)
        rows, cols = four.shape
        pieces.append(jnp.sum(four.astype(F32).reshape(rows // 16, 16, cols), axis=1) * (1.0 / 16))
    unit_ref[...] = jnp.concatenate(pieces, axis=0).astype(BF)


def coarse_rows(xl, k, v):
    rows, cols = k.shape[0], k.shape[1] // 2
    width = 512
    own, send = (pl.BlockSpec((rows, width), column(width, other)) for other in (False, True))
    return pl.pallas_call(
        coarse_kernel,
        grid_spec=pltpu.PrefetchScalarGridSpec(
            num_scalar_prefetch=1,
            grid=(cols // width,),
            in_specs=[own, send, own, send],
            out_specs=pl.BlockSpec((16, width), lambda c, xl: (0, c)),
            scratch_shapes=[pltpu.VMEM((width // D, rows, D), F32)],
        ),
        out_shape=jax.ShapeDtypeStruct((16, cols), BF),
        compiler_params=VMEM,
        cost_estimate=taking(3),
    )(xl, k, k, v, v)


def pool_kernel(xl, k_ref, v_ref, got_ref, up_ref, down_ref, mid_ref, far_ref, scratch):
    low = xl[0] == 0
    for i, ref in enumerate((k_ref, v_ref)):
        own, got = ref[...], got_ref[i]
        first = jnp.where(low, own, got)
        second = jnp.where(low, got, own)
        mid_first = halved(first.astype(F32), scratch)
        mid_second = halved(second.astype(F32), scratch)
        far_first = halved(mid_first.astype(F32), scratch)
        far_second = halved(mid_second.astype(F32), scratch)
        mid_ref[i, 0:128] = mid_first
        mid_ref[i, 128:256] = mid_second
        far_ref[i, 0:64] = far_first
        far_ref[i, 64:128] = far_second
        up_ref[i, 0:128] = second[128:256]
        up_ref[i, 128:192] = mid_first[64:128]
        up_ref[i, 192:256] = mid_second[0:64]
        up_ref[i, 256:288] = far_first[0:32]
        down_ref[i, 0:128] = first[0:128]
        down_ref[i, 128:192] = mid_first[64:128]
        down_ref[i, 192:256] = mid_second[0:64]
        down_ref[i, 256:288] = far_second[32:64]


def pooled(xl, k, v, got):
    _, rows, cols = got.shape
    width = 256
    sizes = (288, 288, 256, 128)
    own = pl.BlockSpec((rows, width), column(width))
    return pl.pallas_call(
        pool_kernel,
        grid_spec=pltpu.PrefetchScalarGridSpec(
            num_scalar_prefetch=1,
            grid=(cols // width,),
            in_specs=[own, own, pl.BlockSpec((2, rows, width), lambda c, xl: (0, 0, c))],
            out_specs=[pl.BlockSpec((2, n, width), lambda c, xl: (0, 0, c)) for n in sizes],
            scratch_shapes=[pltpu.VMEM((width // D, rows, D), F32)],
        ),
        out_shape=[jax.ShapeDtypeStruct((2, n, cols), BF) for n in sizes],
        compiler_params=VMEM, cost_estimate=taking(5),
    )(xl, k, v, got)


def forward_kernel(below_ref, above_ref, up_ref, down_ref, near_ref, scratch):
    below, above = below_ref[0], above_ref[0]
    below_near = halved(below[0:128].astype(F32), scratch)
    above_near = halved(above[0:128].astype(F32), scratch)
    near_ref[0, 0:64] = below_near
    near_ref[0, 64:128] = above_near
    up_ref[0, 0:32] = below[256:288]
    up_ref[0, 32:128] = halved(jnp.concatenate([below[128:256], below_near], axis=0).astype(F32), scratch)
    down_ref[0, 0:96] = halved(jnp.concatenate([above_near, above[128:256]], axis=0).astype(F32), scratch)
    down_ref[0, 96:128] = above[256:288]


def forwarded(below, above):
    _, rows, cols = below.shape
    width = 512
    return pl.pallas_call(
        forward_kernel,
        grid=(2, cols // width),
        in_specs=[pl.BlockSpec((1, rows, width), lambda i, c: (i, 0, c))] * 2,
        out_specs=[pl.BlockSpec((1, 128, width), lambda i, c: (i, 0, c))] * 3,
        out_shape=[jax.ShapeDtypeStruct((2, 128, cols), BF)] * 3,
        scratch_shapes=[pltpu.VMEM((width // D, 192, D), F32)],
        compiler_params=VMEM, cost_estimate=taking(4),
    )(below, above)


def flags(blocks, first, unit, ref):
    ny, nz = lax.axis_size("y"), lax.axis_size("z")
    at = 4 * (lax.axis_index("y") * nz + lax.axis_index("z"))
    block = first + lax.broadcasted_iota(jnp.int32, (blocks * unit, D), 0) // unit + at
    ref[:, D : 2 * D] = jnp.where((block >= 0) & (block < 4 * ny * nz), 1.0, 0.0).astype(BF)


def present():
    ny, nz = lax.axis_size("y"), lax.axis_size("z")
    zz = lax.axis_index("y") * nz + lax.axis_index("z")
    return [zz >= n for n in range(4)], [zz <= ny * nz - 1 - n for n in range(4)]


def put(ref, start, rows, here, fallback):
    ref[start : start + rows.shape[0], 0:D] = rows if fallback is None else jnp.where(here, rows, fallback)


def scores(q, key):
    return lax.dot_general(q, key, (((1,), (1,)), ((), ())), preferred_element_type=F32)


def weighted(parts, top):
    total = jnp.zeros((BLOCK, 2 * D), F32)
    for s, value, size, keep in parts:
        weights = jnp.exp2(s * SCALE - (top - size)).astype(BF)
        if keep is not None:
            weights = weights * keep
        total = total + jnp.dot(weights, value, preferred_element_type=F32)
    return total


def top_of(parts):
    return functools.reduce(
        jnp.maximum, [jnp.max(s, axis=1, keepdims=True) * SCALE + size for s, _, size, _ in parts]
    )


def near_kernel(
    xl, q_own, q_got, k_own, v_own, kv_got, mid, below1, above1, near, coarse0, coarse1, coarse2, coarse3,
    out, stat, kf, vf, km, vm, kc, vc, mask,
):
    low = xl[0] == 0
    coarse_n = mask.shape[1]

    @pl.when(pl.program_id(0) == 0)
    def _():
        flags(6, -1, 128, vf)
        flags(10, -3, 64, vm)
        vc[:, D : 2 * D] = jnp.ones((coarse_n, D), BF)
        y, z = lax.axis_index("y"), lax.axis_index("z")
        ny, nz = lax.axis_size("y"), lax.axis_size("z")
        at = lax.broadcasted_iota(jnp.int32, (16, coarse_n), 1)
        turn = at // (8 * nz)
        other_y = (y + jnp.where(turn == 0, 0, jnp.where(turn == 1, ny - 1, jnp.where(turn == 2, 1, 2)))) % ny
        other_z = (at // 8) % nz
        block = (other_y * nz + other_z) * 4 + (at % 8) // 2
        for b in range(4):
            gap = jnp.abs(block - (4 * (y * nz + z) + b))
            mask[b * 16 : (b + 1) * 16, :] = jnp.where(gap > FAR_REACH, 1.0, 0.0).astype(BF)

    has, has_up = present()
    for i, (own_ref, fine_w, mid_w) in enumerate(((k_own, kf, km), (v_own, vf, vm))):
        is_key = i == 0
        own, got = own_ref[...], kv_got[i]
        first, second = jnp.where(low, own, got), jnp.where(low, got, own)
        fine_w[128:384, 0:D] = first
        fine_w[384:640, 0:D] = second
        put(fine_w, 0, below1[i, 0:128], has[1], first[0:128] if is_key else None)
        put(fine_w, 640, above1[i, 0:128], has_up[1], second[128:256] if is_key else None)
        mid_w[192:448, 0:D] = mid[i]
        m0 = mid[i, 0:64] if is_key else None
        m3 = mid[i, 192:256] if is_key else None
        put(mid_w, 0, below1[i, 128:192], has[1], m0)
        put(mid_w, 64, below1[i, 192:256], has[1], m0)
        put(mid_w, 128, near[i, 0:64], has[1], m0)
        put(mid_w, 448, near[i, 64:128], has_up[1], m3)
        put(mid_w, 512, above1[i, 128:192], has_up[1], m3)
        put(mid_w, 576, above1[i, 192:256], has_up[1], m3)
    step = coarse_n // 4
    for t, part in enumerate((coarse0, coarse1, coarse2, coarse3)):
        kc[t * step : (t + 1) * step] = part[0]
        vc[t * step : (t + 1) * step, 0:D] = part[1]
    qo, qg = q_own[...], q_got[...]
    queries = (jnp.where(low, qo, qg), jnp.where(low, qg, qo))
    left = lax.broadcasted_iota(jnp.int32, (BLOCK, D), 1) < D // 2
    for b in range(4):
        q = queries[b // 2][(b % 2) * 128 : (b % 2 + 1) * 128]
        lo, up = b * 64, (b + 5) * 64
        parts = [
            (scores(q, kf[b * 128 : b * 128 + 384]), vf[b * 128 : b * 128 + 384], 0.0, None),
            (scores(q, km[lo : lo + 128]), vm[lo : lo + 128], 1.0, None),
            (scores(q, km[up : up + 128]), vm[up : up + 128], 1.0, None),
            (scores(q, kc[...]), vc[...], 6.0, mask[b * 16 : b * 16 + 1, :]),
        ]
        top = top_of(parts)
        total = weighted(parts, top)
        out[b * 128 : (b + 1) * 128] = total[:, 0:D]
        stat[b * 128 : (b + 1) * 128] = jnp.where(left, top, total[:, D : 2 * D])


def far_kernel(
    xl, q_own, q_got, far, up, down, below2, above2, below3, above3, near_out, near_stat,
    own_out, send_out, kr, vr, kfar, vfar,
):
    low = xl[0] == 0

    @pl.when(pl.program_id(0) == 0)
    def _():
        flags(22, -9, 32, vr)

    has, has_up = present()
    for i, far_w in enumerate((kr, vr)):
        is_key = i == 0
        far_w[288:416, 0:D] = far[i]
        f0 = far[i, 0:32] if is_key else None
        f3 = far[i, 96:128] if is_key else None
        f0_4 = jnp.concatenate([f0] * 4, axis=0) if is_key else None
        f3_4 = jnp.concatenate([f3] * 4, axis=0) if is_key else None
        put(far_w, 0, below3[i], has[3], f0)
        put(far_w, 32, below2[i], has[2], f0_4)
        put(far_w, 160, up[i], has[1], f0_4)
        put(far_w, 416, down[i], has_up[1], f3_4)
        put(far_w, 544, above2[i], has_up[2], f3_4)
        put(far_w, 672, above3[i], has_up[3], f3)
    qo, qg = q_own[...], q_got[...]
    queries = (jnp.where(low, qo, qg), jnp.where(low, qg, qo))
    results = []
    for b in range(4):
        q = queries[b // 2][(b % 2) * 128 : (b % 2 + 1) * 128]
        kfar[b, 0:192] = kr[b * 32 : b * 32 + 192]
        kfar[b, 192:384] = kr[(b + 13) * 32 : (b + 13) * 32 + 192]
        vfar[b, 0:192] = vr[b * 32 : b * 32 + 192]
        vfar[b, 192:384] = vr[(b + 13) * 32 : (b + 13) * 32 + 192]
        parts = [(scores(q, kfar[b]), vfar[b], 2.0, None)]
        here = slice(b * 128, (b + 1) * 128)
        near_top, near_sum = near_stat[here, 0:1], near_stat[here, D - 1 : D]
        top = jnp.maximum(top_of(parts), near_top)
        total = weighted(parts, top)
        scale = jnp.exp2(near_top - top)
        upper = total[:, 0:D] + near_out[here] * scale
        results.append((upper / (total[:, D : 2 * D] + near_sum * scale)).astype(BF))
    out_first = jnp.concatenate(results[0:2], axis=0)
    out_second = jnp.concatenate(results[2:4], axis=0)
    own_out[...] = jnp.where(low, out_first, out_second)
    send_out[...] = jnp.where(low, out_second, out_first)


def by_head(a):
    lead = a.shape[:-1]
    return pl.BlockSpec(lead + (D,), lambda h, xl, n=len(lead): (0,) * n + (h,))


def attend_call(kernel, xl, own, arrays, outs, out_specs, scratch, cost):
    rows, cols = own[0].shape[0], own[0].shape[1] // 2
    spec_own = pl.BlockSpec((rows, D), column(D))
    order = [(own[0], spec_own), (arrays[0], by_head(arrays[0]))]
    order += [(a, spec_own) for a in own[1:]] + [(a, by_head(a)) for a in arrays[1:]]
    return pl.pallas_call(
        kernel,
        grid_spec=pltpu.PrefetchScalarGridSpec(
            num_scalar_prefetch=1,
            grid=(cols // D,),
            in_specs=[spec for _, spec in order],
            out_specs=out_specs,
            scratch_shapes=scratch,
        ),
        out_shape=outs,
        compiler_params=VMEM,
        cost_estimate=taking(cost),
    )(xl, *(a for a, _ in order))


def attend_near(xl, q, q_got, k, v, arrays):
    rows, cols = q.shape[0], q.shape[1] // 2
    outs = [jax.ShapeDtypeStruct((2 * rows, cols), F32)] * 2
    coarse_n = 4 * arrays[-1].shape[1]
    scratch = [
        pltpu.VMEM((768, D), BF), pltpu.VMEM((768, 2 * D), BF),
        pltpu.VMEM((640, D), BF), pltpu.VMEM((640, 2 * D), BF),
        pltpu.VMEM((coarse_n, D), BF), pltpu.VMEM((coarse_n, 2 * D), BF),
        pltpu.VMEM((64, coarse_n), BF),
    ]
    return attend_call(
        near_kernel, xl, (q, k, v), (q_got, *arrays), outs, [by_head(a) for a in outs], scratch, 16
    )


def attend_far(xl, q, q_got, arrays):
    rows, cols = q.shape[0], q.shape[1] // 2
    outs = [jax.ShapeDtypeStruct((rows, 2 * cols), BF), jax.ShapeDtypeStruct((rows, cols), BF)]
    scratch = [
        pltpu.VMEM((704, D), BF), pltpu.VMEM((704, 2 * D), BF),
        pltpu.VMEM((4, 384, D), BF), pltpu.VMEM((4, 384, 2 * D), BF),
    ]
    return attend_call(
        far_kernel, xl, (q,), (q_got, *arrays), outs,
        [pl.BlockSpec((rows, D), column(D)), by_head(outs[1])], scratch, 9,
    )


def moved(a, axis, step):
    n = lax.axis_size(axis)
    return lax.ppermute(a, axis, [(i, (i + step) % n) for i in range(n)])


def shifted(a, step):
    n = lax.axis_size(YZ)
    return lax.ppermute(a, YZ, [(i, i + step) for i in range(n) if 0 <= i + step < n])


def per_device(queries, key_rows, value_rows):
    xl = lax.axis_index("xl")
    low = xl == 0
    at = xl.reshape(1)
    half = queries.shape[1] // 2

    def theirs(a):
        return lax.dynamic_slice_in_dim(a, (1 - xl) * half, half, a.ndim - 1)

    def swapped(a):
        return moved(a, "xl", 1)

    kv_send, keys, values = lax.optimization_barrier(
        (jnp.stack([theirs(key_rows), theirs(value_rows)]), key_rows, value_rows)
    )
    kv_got = swapped(kv_send)
    unit = coarse_rows(at, keys, values)
    unit_got = swapped(unit)
    kept = unit.reshape(2, 8, half)[:, 0:4]
    came = unit_got.reshape(2, 8, half)[:, 4:8]
    unit = jnp.concatenate([jnp.where(low, kept, came), jnp.where(low, came, kept)], axis=1).reshape(16, half)
    units = lax.all_gather(unit, "z")
    units = jnp.moveaxis(units.reshape(-1, 2, 8, half), 1, 0).reshape(2, -1, half)
    q_got = swapped(theirs(queries))
    kv_got, units, q_got = lax.optimization_barrier((kv_got, units, q_got))
    up1, down1, mid, far = pooled(at, key_rows, value_rows, kv_got)
    up1, down1, units = lax.optimization_barrier((up1, down1, units))
    below1, above1 = shifted(up1, 1), shifted(down1, -1)
    coarse = (units, moved(units, "y", 1), moved(units, "y", -1), moved(units, "y", 2))
    below3, above3 = shifted(far[:, 96:128], 3), shifted(far[:, 0:32], -3)
    up, down, near = forwarded(below1, above1)
    below2, above2 = shifted(up, 1), shifted(down, -1)
    near_out, near_stat = attend_near(
        at, queries, q_got, key_rows, value_rows, (kv_got, mid, below1, above1, near, *coarse)
    )
    out, send_out = attend_far(
        at, queries, q_got, (far, up, down, below2, above2, below3, above3, near_out, near_stat)
    )
    return lax.dynamic_update_slice_in_dim(out, swapped(send_out), (1 - xl) * half, 1)


def solution(mesh):
    torus = Mesh(
        mesh.devices.reshape(4, 16, 2, mesh.shape["head"]), ("y", "z", "xl", "head")
    )
    spec = P(SEQ, "head")
    return jax.shard_map(
        per_device, mesh=torus, in_specs=(spec, spec, spec), out_specs=spec, check_vma=False
    )
```

```python
import functools
import math

import jax
import jax.numpy as jnp
from jax import lax
from jax.experimental import pallas as pl
from jax.experimental.pallas import tpu as pltpu
from jax.sharding import Mesh
from jax.sharding import PartitionSpec as P

D = 128
BLOCK = 128
FAR_REACH = 9
SEQ = ("y", "z", "xl")
YZ = ("y", "z")
Z = "z"
BF = jnp.bfloat16
F32 = jnp.float32
SCALE = math.log2(math.e) / math.sqrt(D)
VMEM = pltpu.CompilerParams(vmem_limit_bytes=58 * 2**20)


def taking(microseconds):
    return pl.CostEstimate(flops=0, bytes_accessed=int(microseconds * 3.6e6), transcendentals=0)


def halved(x, scratch):
    rows, cols = x.shape
    parts = []
    for c in range(cols // D):
        scratch[c, 0:rows] = x[:, c * D : (c + 1) * D]
        even = scratch[c, pl.ds(0, rows // 2, stride=2)]
        odd = scratch[c, pl.ds(1, rows // 2, stride=2)]
        parts.append((0.5 * (even + odd)).astype(BF))
    return parts[0] if len(parts) == 1 else jnp.concatenate(parts, axis=1)


def column(width, other=False):
    n = 8 * D // width

    def index(i, xl):
        return (0, (1 - xl[0] if other else xl[0]) * n + i)

    return index


def coarse_kernel(xl, k_own, k_send, v_own, v_send, unit_ref, scratch):
    pieces = []
    for ref in (k_own, k_send, v_own, v_send):
        four = halved(halved(ref[...].astype(F32), scratch).astype(F32), scratch)
        rows, cols = four.shape
        pieces.append(jnp.sum(four.astype(F32).reshape(rows // 16, 16, cols), axis=1) * (1.0 / 16))
    unit_ref[...] = jnp.concatenate(pieces, axis=0).astype(BF)


def coarse_rows(xl, k, v):
    rows, cols = k.shape[0], k.shape[1] // 2
    width = 512
    own, send = (pl.BlockSpec((rows, width), column(width, other)) for other in (False, True))
    return pl.pallas_call(
        coarse_kernel,
        grid_spec=pltpu.PrefetchScalarGridSpec(
            num_scalar_prefetch=1,
            grid=(cols // width,),
            in_specs=[own, send, own, send],
            out_specs=pl.BlockSpec((16, width), lambda c, xl: (0, c)),
            scratch_shapes=[pltpu.VMEM((width // D, rows, D), F32)],
        ),
        out_shape=jax.ShapeDtypeStruct((16, cols), BF),
        compiler_params=VMEM,
        cost_estimate=taking(3),
    )(xl, k, k, v, v)


def pool_kernel(xl, k_ref, v_ref, got_ref, up_ref, down_ref, mid_ref, far_ref, scratch):
    low = xl[0] == 0
    for i, ref in enumerate((k_ref, v_ref)):
        own, got = ref[...], got_ref[i]
        first = jnp.where(low, own, got)
        second = jnp.where(low, got, own)
        mid_first = halved(first.astype(F32), scratch)
        mid_second = halved(second.astype(F32), scratch)
        far_first = halved(mid_first.astype(F32), scratch)
        far_second = halved(mid_second.astype(F32), scratch)
        mid_ref[i, 0:128] = mid_first
        mid_ref[i, 128:256] = mid_second
        far_ref[i, 0:64] = far_first
        far_ref[i, 64:128] = far_second
        up_ref[i, 0:128] = second[128:256]
        up_ref[i, 128:192] = mid_first[64:128]
        up_ref[i, 192:256] = mid_second[0:64]
        up_ref[i, 256:288] = far_first[0:32]
        down_ref[i, 0:128] = first[0:128]
        down_ref[i, 128:192] = mid_first[64:128]
        down_ref[i, 192:256] = mid_second[0:64]
        down_ref[i, 256:288] = far_second[32:64]


def pooled(xl, k, v, got):
    _, rows, cols = got.shape
    width = 256
    sizes = (288, 288, 256, 128)
    own = pl.BlockSpec((rows, width), column(width))
    return pl.pallas_call(
        pool_kernel,
        grid_spec=pltpu.PrefetchScalarGridSpec(
            num_scalar_prefetch=1,
            grid=(cols // width,),
            in_specs=[own, own, pl.BlockSpec((2, rows, width), lambda c, xl: (0, 0, c))],
            out_specs=[pl.BlockSpec((2, n, width), lambda c, xl: (0, 0, c)) for n in sizes],
            scratch_shapes=[pltpu.VMEM((width // D, rows, D), F32)],
        ),
        out_shape=[jax.ShapeDtypeStruct((2, n, cols), BF) for n in sizes],
        compiler_params=VMEM, cost_estimate=taking(5),
    )(xl, k, v, got)


def forward_kernel(below_ref, above_ref, up_ref, down_ref, near_ref, scratch):
    below, above = below_ref[0], above_ref[0]
    below_near = halved(below[0:128].astype(F32), scratch)
    above_near = halved(above[0:128].astype(F32), scratch)
    near_ref[0, 0:64] = below_near
    near_ref[0, 64:128] = above_near
    up_ref[0, 0:32] = below[256:288]
    up_ref[0, 32:128] = halved(jnp.concatenate([below[128:256], below_near], axis=0).astype(F32), scratch)
    down_ref[0, 0:96] = halved(jnp.concatenate([above_near, above[128:256]], axis=0).astype(F32), scratch)
    down_ref[0, 96:128] = above[256:288]


def forwarded(below, above):
    _, rows, cols = below.shape
    width = 512
    return pl.pallas_call(
        forward_kernel,
        grid=(2, cols // width),
        in_specs=[pl.BlockSpec((1, rows, width), lambda i, c: (i, 0, c))] * 2,
        out_specs=[pl.BlockSpec((1, 128, width), lambda i, c: (i, 0, c))] * 3,
        out_shape=[jax.ShapeDtypeStruct((2, 128, cols), BF)] * 3,
        scratch_shapes=[pltpu.VMEM((width // D, 192, D), F32)],
        compiler_params=VMEM, cost_estimate=taking(4),
    )(below, above)


def flags(blocks, first, unit, ref):
    ny, nz = lax.axis_size("y"), lax.axis_size("z")
    at = 4 * (lax.axis_index("y") * nz + lax.axis_index("z"))
    block = first + lax.broadcasted_iota(jnp.int32, (blocks * unit, D), 0) // unit + at
    ref[:, D : 2 * D] = jnp.where((block >= 0) & (block < 4 * ny * nz), 1.0, 0.0).astype(BF)


def present():
    ny, nz = lax.axis_size("y"), lax.axis_size("z")
    zz = lax.axis_index("y") * nz + lax.axis_index("z")
    return [zz >= n for n in range(4)], [zz <= ny * nz - 1 - n for n in range(4)]


def put(ref, start, rows, here, fallback):
    ref[start : start + rows.shape[0], 0:D] = rows if fallback is None else jnp.where(here, rows, fallback)


def scores(q, key):
    return lax.dot_general(q, key, (((1,), (1,)), ((), ())), preferred_element_type=F32)


def weighted(parts, top):
    total = jnp.zeros((BLOCK, 2 * D), F32)
    for s, value, size, keep in parts:
        weights = jnp.exp2(s * SCALE - (top - size)).astype(BF)
        if keep is not None:
            weights = weights * keep
        total = total + jnp.dot(weights, value, preferred_element_type=F32)
    return total


def top_of(parts):
    return functools.reduce(
        jnp.maximum, [jnp.max(s, axis=1, keepdims=True) * SCALE + size for s, _, size, _ in parts]
    )


def near_kernel(xl, q_own, q_got, k_own, v_own, kv_got, mid, below1, above1, near, out, stat, kf, vf, km, vm):
    low = xl[0] == 0

    @pl.when(pl.program_id(0) == 0)
    def _():
        flags(6, -1, 128, vf)
        flags(10, -3, 64, vm)

    has, has_up = present()
    for i, (own_ref, fine_w, mid_w) in enumerate(((k_own, kf, km), (v_own, vf, vm))):
        is_key = i == 0
        own, got = own_ref[...], kv_got[i]
        first, second = jnp.where(low, own, got), jnp.where(low, got, own)
        fine_w[128:384, 0:D] = first
        fine_w[384:640, 0:D] = second
        put(fine_w, 0, below1[i, 0:128], has[1], first[0:128] if is_key else None)
        put(fine_w, 640, above1[i, 0:128], has_up[1], second[128:256] if is_key else None)
        mid_w[192:448, 0:D] = mid[i]
        m0 = mid[i, 0:64] if is_key else None
        m3 = mid[i, 192:256] if is_key else None
        put(mid_w, 0, below1[i, 128:192], has[1], m0)
        put(mid_w, 64, below1[i, 192:256], has[1], m0)
        put(mid_w, 128, near[i, 0:64], has[1], m0)
        put(mid_w, 448, near[i, 64:128], has_up[1], m3)
        put(mid_w, 512, above1[i, 128:192], has_up[1], m3)
        put(mid_w, 576, above1[i, 192:256], has_up[1], m3)
    qo, qg = q_own[...], q_got[...]
    queries = (jnp.where(low, qo, qg), jnp.where(low, qg, qo))
    left = lax.broadcasted_iota(jnp.int32, (BLOCK, D), 1) < D // 2
    for b in range(4):
        q = queries[b // 2][(b % 2) * 128 : (b % 2 + 1) * 128]
        lo, up = b * 64, (b + 5) * 64
        parts = [
            (scores(q, kf[b * 128 : b * 128 + 384]), vf[b * 128 : b * 128 + 384], 0.0, None),
            (scores(q, km[lo : lo + 128]), vm[lo : lo + 128], 1.0, None),
            (scores(q, km[up : up + 128]), vm[up : up + 128], 1.0, None),
        ]
        top = top_of(parts)
        total = weighted(parts, top)
        out[b * 128 : (b + 1) * 128] = total[:, 0:D]
        stat[b * 128 : (b + 1) * 128] = jnp.where(left, top, total[:, D : 2 * D])


def far_kernel(
    xl, q_own, q_got, far, up, down, below2, above2, below3, above3, coarse0, coarse1, near_out, near_stat,
    own_out, send_out, kr, vr, kc, vc, kfar, vfar, mask,
):
    low = xl[0] == 0
    y = lax.axis_index("y")
    ny, nz = lax.axis_size("y"), lax.axis_size("z")
    coarse_n = 2 * coarse0.shape[1]

    @pl.when(pl.program_id(0) == 0)
    def _():
        flags(22, -9, 32, vr)
        vc[:, D : 2 * D] = jnp.ones((coarse_n, D), BF)
        for b in range(4):
            at = lax.broadcasted_iota(jnp.int32, (16, coarse_n), 1)
            turn = at // (8 * nz)
            other = jnp.where(turn < 2, y, ny - 1 - y)
            other = jnp.where(turn % 2 == 0, other, other + 1 - 2 * (other % 2))
            block = (other * nz + (at // 8) % nz) * 4 + (at % 8) // 2
            gap = jnp.abs(block - (4 * (y * nz + lax.axis_index("z")) + b))
            mask[b * 16 : (b + 1) * 16, :] = jnp.where(gap > FAR_REACH, 1.0, 0.0).astype(BF)

    has, has_up = present()
    for i, far_w in enumerate((kr, vr)):
        is_key = i == 0
        far_w[288:416, 0:D] = far[i]
        f0 = far[i, 0:32] if is_key else None
        f3 = far[i, 96:128] if is_key else None
        f0_4 = jnp.concatenate([f0] * 4, axis=0) if is_key else None
        f3_4 = jnp.concatenate([f3] * 4, axis=0) if is_key else None
        put(far_w, 0, below3[i], has[3], f0)
        put(far_w, 32, below2[i], has[2], f0_4)
        put(far_w, 160, up[i], has[1], f0_4)
        put(far_w, 416, down[i], has_up[1], f3_4)
        put(far_w, 544, above2[i], has_up[2], f3_4)
        put(far_w, 672, above3[i], has_up[3], f3)
    step = coarse_n // 2
    for t, part in enumerate((coarse0, coarse1)):
        kc[t * step : (t + 1) * step] = part[0]
        vc[t * step : (t + 1) * step, 0:D] = part[1]
    qo, qg = q_own[...], q_got[...]
    queries = (jnp.where(low, qo, qg), jnp.where(low, qg, qo))
    results = []
    for b in range(4):
        q = queries[b // 2][(b % 2) * 128 : (b % 2 + 1) * 128]
        kfar[0:192] = kr[b * 32 : b * 32 + 192]
        kfar[192:384] = kr[(b + 13) * 32 : (b + 13) * 32 + 192]
        vfar[0:192] = vr[b * 32 : b * 32 + 192]
        vfar[192:384] = vr[(b + 13) * 32 : (b + 13) * 32 + 192]
        parts = [
            (scores(q, kfar[...]), vfar[...], 2.0, None),
            (scores(q, kc[...]), vc[...], 6.0, mask[b * 16 : b * 16 + 1, :]),
        ]
        here = slice(b * 128, (b + 1) * 128)
        near_top, near_sum = near_stat[here, 0:1], near_stat[here, D - 1 : D]
        top = jnp.maximum(top_of(parts), near_top)
        total = weighted(parts, top)
        scale = jnp.exp2(near_top - top)
        upper = total[:, 0:D] + near_out[here] * scale
        results.append((upper / (total[:, D : 2 * D] + near_sum * scale)).astype(BF))
    out_first = jnp.concatenate(results[0:2], axis=0)
    out_second = jnp.concatenate(results[2:4], axis=0)
    own_out[...] = jnp.where(low, out_first, out_second)
    send_out[...] = jnp.where(low, out_second, out_first)


def by_head(a):
    lead = a.shape[:-1]
    return pl.BlockSpec(lead + (D,), lambda h, xl, n=len(lead): (0,) * n + (h,))


def attend_call(kernel, xl, own, arrays, outs, out_specs, scratch, cost):
    rows, cols = own[0].shape[0], own[0].shape[1] // 2
    spec_own = pl.BlockSpec((rows, D), column(D))
    order = [(own[0], spec_own), (arrays[0], by_head(arrays[0]))]
    order += [(a, spec_own) for a in own[1:]] + [(a, by_head(a)) for a in arrays[1:]]
    return pl.pallas_call(
        kernel,
        grid_spec=pltpu.PrefetchScalarGridSpec(
            num_scalar_prefetch=1,
            grid=(cols // D,),
            in_specs=[spec for _, spec in order],
            out_specs=out_specs,
            scratch_shapes=scratch,
        ),
        out_shape=outs,
        compiler_params=VMEM,
        cost_estimate=taking(cost),
    )(xl, *(a for a, _ in order))


def attend_near(xl, q, q_got, k, v, arrays):
    rows, cols = q.shape[0], q.shape[1] // 2
    outs = [jax.ShapeDtypeStruct((2 * rows, cols), F32)] * 2
    scratch = [
        pltpu.VMEM((768, D), BF), pltpu.VMEM((768, 2 * D), BF),
        pltpu.VMEM((640, D), BF), pltpu.VMEM((640, 2 * D), BF),
    ]
    return attend_call(
        near_kernel, xl, (q, k, v), (q_got, *arrays), outs, [by_head(a) for a in outs], scratch, 12
    )


def attend_far(xl, q, q_got, arrays):
    rows, cols = q.shape[0], q.shape[1] // 2
    outs = [jax.ShapeDtypeStruct((rows, 2 * cols), BF), jax.ShapeDtypeStruct((rows, cols), BF)]
    coarse_n = 2 * arrays[7].shape[1]
    scratch = [
        pltpu.VMEM((704, D), BF), pltpu.VMEM((704, 2 * D), BF),
        pltpu.VMEM((coarse_n, D), BF), pltpu.VMEM((coarse_n, 2 * D), BF),
        pltpu.VMEM((384, D), BF), pltpu.VMEM((384, 2 * D), BF),
        pltpu.VMEM((64, coarse_n), BF),
    ]
    return attend_call(
        far_kernel, xl, (q,), (q_got, *arrays), outs,
        [pl.BlockSpec((rows, D), column(D)), by_head(outs[1])], scratch, 15,
    )


def moved(a, axis, step):
    n = lax.axis_size(axis)
    return lax.ppermute(a, axis, [(i, (i + step) % n) for i in range(n)])


def shifted(a, step):
    n = lax.axis_size(YZ)
    return lax.ppermute(a, YZ, [(i, i + step) for i in range(n) if 0 <= i + step < n])


def per_device(queries, key_rows, value_rows):
    xl = lax.axis_index("xl")
    low = xl == 0
    at = xl.reshape(1)
    half = queries.shape[1] // 2

    def theirs(a):
        return lax.dynamic_slice_in_dim(a, (1 - xl) * half, half, a.ndim - 1)

    def swapped(a):
        return moved(a, "xl", 1)

    unit = coarse_rows(at, key_rows, value_rows)
    unit_got = swapped(unit)
    kv_send = jnp.stack([theirs(key_rows), theirs(value_rows)])
    kv_send, q_send, unit_got = lax.optimization_barrier((kv_send, theirs(queries), unit_got))
    kv_got, q_got = swapped(kv_send), swapped(q_send)
    kept = unit.reshape(2, 8, half)[:, 0:4]
    came = unit_got.reshape(2, 8, half)[:, 4:8]
    unit = jnp.concatenate([jnp.where(low, kept, came), jnp.where(low, came, kept)], axis=1).reshape(16, half)
    units = lax.all_gather(unit, "z")
    units = jnp.moveaxis(units.reshape(-1, 2, 8, half), 1, 0).reshape(2, -1, half)
    kv_got, units, q_got = lax.optimization_barrier((kv_got, units, q_got))
    up1, down1, mid, far = pooled(at, key_rows, value_rows, kv_got)
    up1, down1, units = lax.optimization_barrier((up1, down1, units))
    below1, above1 = shifted(up1, 1), shifted(down1, -1)
    ny = lax.axis_size("y")
    coarse0 = jnp.concatenate([units, lax.ppermute(units, "y", [(i, i ^ 1) for i in range(ny)])], axis=1)
    coarse1 = lax.ppermute(coarse0, "y", [(i, ny - 1 - i) for i in range(ny)])
    below3, above3 = shifted(far[:, 96:128], 3), shifted(far[:, 0:32], -3)
    up, down, near = forwarded(below1, above1)
    below2, above2 = shifted(up, 1), shifted(down, -1)
    near_out, near_stat = attend_near(
        at, queries, q_got, key_rows, value_rows, (kv_got, mid, below1, above1, near)
    )
    out, send_out = attend_far(
        at, queries, q_got,
        (far, up, down, below2, above2, below3, above3, coarse0, coarse1, near_out, near_stat),
    )
    return lax.dynamic_update_slice_in_dim(out, swapped(send_out), (1 - xl) * half, 1)


def solution(mesh):
    torus = Mesh(
        mesh.devices.reshape(4, 16, 2, mesh.shape["head"]), ("y", "z", "xl", "head")
    )
    spec = P(SEQ, "head")
    return jax.shard_map(
        per_device, mesh=torus, in_specs=(spec, spec, spec), out_specs=spec, check_vma=False
    )
```

```python
import functools
import math

import jax
import jax.numpy as jnp
from jax import lax
from jax.experimental import pallas as pl
from jax.experimental.pallas import tpu as pltpu
from jax.sharding import Mesh
from jax.sharding import PartitionSpec as P

D = 128
BLOCK = 128
FAR_REACH = 9
SEQ = ("y", "z", "xl")
YZ = ("y", "z")
Z = "z"
BF = jnp.bfloat16
F32 = jnp.float32
SCALE = math.log2(math.e) / math.sqrt(D)
VMEM = pltpu.CompilerParams(vmem_limit_bytes=58 * 2**20)


def taking(microseconds):
    return pl.CostEstimate(flops=0, bytes_accessed=int(microseconds * 3.6e6), transcendentals=0)


def halved(x, scratch):
    rows, cols = x.shape
    parts = []
    for c in range(cols // D):
        scratch[c, 0:rows] = x[:, c * D : (c + 1) * D]
        even = scratch[c, pl.ds(0, rows // 2, stride=2)]
        odd = scratch[c, pl.ds(1, rows // 2, stride=2)]
        parts.append((0.5 * (even + odd)).astype(BF))
    return parts[0] if len(parts) == 1 else jnp.concatenate(parts, axis=1)


def column(width, other=False):
    n = 8 * D // width

    def index(i, xl):
        return (0, (1 - xl[0] if other else xl[0]) * n + i)

    return index


def coarse_kernel(xl, k_own, k_send, v_own, v_send, unit_ref, scratch):
    pieces = []
    for ref in (k_own, k_send, v_own, v_send):
        four = halved(halved(ref[...].astype(F32), scratch).astype(F32), scratch)
        rows, cols = four.shape
        pieces.append(jnp.sum(four.astype(F32).reshape(rows // 16, 16, cols), axis=1) * (1.0 / 16))
    unit_ref[...] = jnp.concatenate(pieces, axis=0).astype(BF)


def coarse_rows(xl, k, v):
    rows, cols = k.shape[0], k.shape[1] // 2
    width = 512
    own, send = (pl.BlockSpec((rows, width), column(width, other)) for other in (False, True))
    return pl.pallas_call(
        coarse_kernel,
        grid_spec=pltpu.PrefetchScalarGridSpec(
            num_scalar_prefetch=1,
            grid=(cols // width,),
            in_specs=[own, send, own, send],
            out_specs=pl.BlockSpec((16, width), lambda c, xl: (0, c)),
            scratch_shapes=[pltpu.VMEM((width // D, rows, D), F32)],
        ),
        out_shape=jax.ShapeDtypeStruct((16, cols), BF),
        compiler_params=VMEM,
        cost_estimate=taking(3),
    )(xl, k, k, v, v)


def pool_kernel(xl, k_ref, v_ref, got_ref, up_ref, down_ref, mid_ref, far_ref, scratch):
    low = xl[0] == 0
    for i, ref in enumerate((k_ref, v_ref)):
        own, got = ref[...], got_ref[i]
        first = jnp.where(low, own, got)
        second = jnp.where(low, got, own)
        mid_first = halved(first.astype(F32), scratch)
        mid_second = halved(second.astype(F32), scratch)
        far_first = halved(mid_first.astype(F32), scratch)
        far_second = halved(mid_second.astype(F32), scratch)
        mid_ref[i, 0:128] = mid_first
        mid_ref[i, 128:256] = mid_second
        far_ref[i, 0:64] = far_first
        far_ref[i, 64:128] = far_second
        up_ref[i, 0:128] = second[128:256]
        up_ref[i, 128:192] = mid_first[64:128]
        up_ref[i, 192:256] = mid_second[0:64]
        up_ref[i, 256:288] = far_first[0:32]
        down_ref[i, 0:128] = first[0:128]
        down_ref[i, 128:192] = mid_first[64:128]
        down_ref[i, 192:256] = mid_second[0:64]
        down_ref[i, 256:288] = far_second[32:64]


def pooled(xl, k, v, got):
    _, rows, cols = got.shape
    width = 256
    sizes = (288, 288, 256, 128)
    own = pl.BlockSpec((rows, width), column(width))
    return pl.pallas_call(
        pool_kernel,
        grid_spec=pltpu.PrefetchScalarGridSpec(
            num_scalar_prefetch=1,
            grid=(cols // width,),
            in_specs=[own, own, pl.BlockSpec((2, rows, width), lambda c, xl: (0, 0, c))],
            out_specs=[pl.BlockSpec((2, n, width), lambda c, xl: (0, 0, c)) for n in sizes],
            scratch_shapes=[pltpu.VMEM((width // D, rows, D), F32)],
        ),
        out_shape=[jax.ShapeDtypeStruct((2, n, cols), BF) for n in sizes],
        compiler_params=VMEM, cost_estimate=taking(5),
    )(xl, k, v, got)


def forward_kernel(below_ref, above_ref, up_ref, down_ref, near_ref, scratch):
    below, above = below_ref[0], above_ref[0]
    below_near = halved(below[0:128].astype(F32), scratch)
    above_near = halved(above[0:128].astype(F32), scratch)
    near_ref[0, 0:64] = below_near
    near_ref[0, 64:128] = above_near
    up_ref[0, 0:32] = below[256:288]
    up_ref[0, 32:128] = halved(jnp.concatenate([below[128:256], below_near], axis=0).astype(F32), scratch)
    down_ref[0, 0:96] = halved(jnp.concatenate([above_near, above[128:256]], axis=0).astype(F32), scratch)
    down_ref[0, 96:128] = above[256:288]


def forwarded(below, above):
    _, rows, cols = below.shape
    width = 512
    return pl.pallas_call(
        forward_kernel,
        grid=(2, cols // width),
        in_specs=[pl.BlockSpec((1, rows, width), lambda i, c: (i, 0, c))] * 2,
        out_specs=[pl.BlockSpec((1, 128, width), lambda i, c: (i, 0, c))] * 3,
        out_shape=[jax.ShapeDtypeStruct((2, 128, cols), BF)] * 3,
        scratch_shapes=[pltpu.VMEM((width // D, 192, D), F32)],
        compiler_params=VMEM, cost_estimate=taking(4),
    )(below, above)


def flags(blocks, first, unit, ref):
    ny, nz = lax.axis_size("y"), lax.axis_size("z")
    at = 4 * (lax.axis_index("y") * nz + lax.axis_index("z"))
    block = first + lax.broadcasted_iota(jnp.int32, (blocks * unit, D), 0) // unit + at
    ref[:, D : 2 * D] = jnp.where((block >= 0) & (block < 4 * ny * nz), 1.0, 0.0).astype(BF)


def present():
    ny, nz = lax.axis_size("y"), lax.axis_size("z")
    zz = lax.axis_index("y") * nz + lax.axis_index("z")
    return [zz >= n for n in range(4)], [zz <= ny * nz - 1 - n for n in range(4)]


def put(ref, start, rows, here, fallback):
    ref[start : start + rows.shape[0], 0:D] = rows if fallback is None else jnp.where(here, rows, fallback)


def scores(q, key):
    return lax.dot_general(q, key, (((1,), (1,)), ((), ())), preferred_element_type=F32)


def weighted(parts, top):
    total = jnp.zeros((BLOCK, 2 * D), F32)
    for s, value, size, keep in parts:
        weights = jnp.exp2(s * SCALE - (top - size)).astype(BF)
        if keep is not None:
            weights = weights * keep
        total = total + jnp.dot(weights, value, preferred_element_type=F32)
    return total


def top_of(parts):
    return functools.reduce(
        jnp.maximum, [jnp.max(s, axis=1, keepdims=True) * SCALE + size for s, _, size, _ in parts]
    )


def near_kernel(xl, q_own, q_got, k_own, v_own, kv_got, mid, below1, above1, near, out, stat, kf, vf, km, vm):
    low = xl[0] == 0

    @pl.when(pl.program_id(0) == 0)
    def _():
        flags(6, -1, 128, vf)
        flags(10, -3, 64, vm)

    has, has_up = present()
    for i, (own_ref, fine_w, mid_w) in enumerate(((k_own, kf, km), (v_own, vf, vm))):
        is_key = i == 0
        own, got = own_ref[...], kv_got[i]
        first, second = jnp.where(low, own, got), jnp.where(low, got, own)
        fine_w[128:384, 0:D] = first
        fine_w[384:640, 0:D] = second
        put(fine_w, 0, below1[i, 0:128], has[1], first[0:128] if is_key else None)
        put(fine_w, 640, above1[i, 0:128], has_up[1], second[128:256] if is_key else None)
        mid_w[192:448, 0:D] = mid[i]
        m0 = mid[i, 0:64] if is_key else None
        m3 = mid[i, 192:256] if is_key else None
        put(mid_w, 0, below1[i, 128:192], has[1], m0)
        put(mid_w, 64, below1[i, 192:256], has[1], m0)
        put(mid_w, 128, near[i, 0:64], has[1], m0)
        put(mid_w, 448, near[i, 64:128], has_up[1], m3)
        put(mid_w, 512, above1[i, 128:192], has_up[1], m3)
        put(mid_w, 576, above1[i, 192:256], has_up[1], m3)
    qo, qg = q_own[...], q_got[...]
    queries = (jnp.where(low, qo, qg), jnp.where(low, qg, qo))
    left = lax.broadcasted_iota(jnp.int32, (BLOCK, D), 1) < D // 2
    for b in range(4):
        q = queries[b // 2][(b % 2) * 128 : (b % 2 + 1) * 128]
        lo, up = b * 64, (b + 5) * 64
        parts = [
            (scores(q, kf[b * 128 : b * 128 + 384]), vf[b * 128 : b * 128 + 384], 0.0, None),
            (scores(q, km[lo : lo + 128]), vm[lo : lo + 128], 1.0, None),
            (scores(q, km[up : up + 128]), vm[up : up + 128], 1.0, None),
        ]
        top = top_of(parts)
        total = weighted(parts, top)
        out[b * 128 : (b + 1) * 128] = total[:, 0:D]
        stat[b * 128 : (b + 1) * 128] = jnp.where(left, top, total[:, D : 2 * D])


def far_kernel(
    xl, q_own, q_got, far, up, down, below2, above2, below3, above3, coarse0, coarse1, coarse2, coarse3, near_out, near_stat,
    own_out, send_out, kr, vr, kc, vc, kfar, vfar, mask,
):
    low = xl[0] == 0
    y = lax.axis_index("y")
    ny, nz = lax.axis_size("y"), lax.axis_size("z")
    coarse_n = 4 * coarse0.shape[1]

    @pl.when(pl.program_id(0) == 0)
    def _():
        flags(22, -9, 32, vr)
        vc[:, D : 2 * D] = jnp.ones((coarse_n, D), BF)
        for b in range(4):
            at = lax.broadcasted_iota(jnp.int32, (16, coarse_n), 1)
            turn = at // (8 * nz)
            other = (y + jnp.where(lax.axis_index("z") < nz // 2, ny - turn, turn)) % ny
            block = (other * nz + (at // 8) % nz) * 4 + (at % 8) // 2
            gap = jnp.abs(block - (4 * (y * nz + lax.axis_index("z")) + b))
            mask[b * 16 : (b + 1) * 16, :] = jnp.where(gap > FAR_REACH, 1.0, 0.0).astype(BF)

    has, has_up = present()
    for i, far_w in enumerate((kr, vr)):
        is_key = i == 0
        far_w[288:416, 0:D] = far[i]
        f0 = far[i, 0:32] if is_key else None
        f3 = far[i, 96:128] if is_key else None
        f0_4 = jnp.concatenate([f0] * 4, axis=0) if is_key else None
        f3_4 = jnp.concatenate([f3] * 4, axis=0) if is_key else None
        put(far_w, 0, below3[i], has[3], f0)
        put(far_w, 32, below2[i], has[2], f0_4)
        put(far_w, 160, up[i], has[1], f0_4)
        put(far_w, 416, down[i], has_up[1], f3_4)
        put(far_w, 544, above2[i], has_up[2], f3_4)
        put(far_w, 672, above3[i], has_up[3], f3)
    step = coarse_n // 4
    for t, part in enumerate((coarse0, coarse1, coarse2, coarse3)):
        kc[t * step : (t + 1) * step] = part[0]
        vc[t * step : (t + 1) * step, 0:D] = part[1]
    qo, qg = q_own[...], q_got[...]
    queries = (jnp.where(low, qo, qg), jnp.where(low, qg, qo))
    results = []
    for b in range(4):
        q = queries[b // 2][(b % 2) * 128 : (b % 2 + 1) * 128]
        kfar[0:192] = kr[b * 32 : b * 32 + 192]
        kfar[192:384] = kr[(b + 13) * 32 : (b + 13) * 32 + 192]
        vfar[0:192] = vr[b * 32 : b * 32 + 192]
        vfar[192:384] = vr[(b + 13) * 32 : (b + 13) * 32 + 192]
        parts = [
            (scores(q, kfar[...]), vfar[...], 2.0, None),
            (scores(q, kc[...]), vc[...], 6.0, mask[b * 16 : b * 16 + 1, :]),
        ]
        here = slice(b * 128, (b + 1) * 128)
        near_top, near_sum = near_stat[here, 0:1], near_stat[here, D - 1 : D]
        top = jnp.maximum(top_of(parts), near_top)
        total = weighted(parts, top)
        scale = jnp.exp2(near_top - top)
        upper = total[:, 0:D] + near_out[here] * scale
        results.append((upper / (total[:, D : 2 * D] + near_sum * scale)).astype(BF))
    out_first = jnp.concatenate(results[0:2], axis=0)
    out_second = jnp.concatenate(results[2:4], axis=0)
    own_out[...] = jnp.where(low, out_first, out_second)
    send_out[...] = jnp.where(low, out_second, out_first)


def by_head(a):
    lead = a.shape[:-1]
    return pl.BlockSpec(lead + (D,), lambda h, xl, n=len(lead): (0,) * n + (h,))


def attend_call(kernel, xl, own, arrays, outs, out_specs, scratch, cost):
    rows, cols = own[0].shape[0], own[0].shape[1] // 2
    spec_own = pl.BlockSpec((rows, D), column(D))
    order = [(own[0], spec_own), (arrays[0], by_head(arrays[0]))]
    order += [(a, spec_own) for a in own[1:]] + [(a, by_head(a)) for a in arrays[1:]]
    return pl.pallas_call(
        kernel,
        grid_spec=pltpu.PrefetchScalarGridSpec(
            num_scalar_prefetch=1,
            grid=(cols // D,),
            in_specs=[spec for _, spec in order],
            out_specs=out_specs,
            scratch_shapes=scratch,
        ),
        out_shape=outs,
        compiler_params=VMEM,
        cost_estimate=taking(cost),
    )(xl, *(a for a, _ in order))


def attend_near(xl, q, q_got, k, v, arrays):
    rows, cols = q.shape[0], q.shape[1] // 2
    outs = [jax.ShapeDtypeStruct((2 * rows, cols), F32)] * 2
    scratch = [
        pltpu.VMEM((768, D), BF), pltpu.VMEM((768, 2 * D), BF),
        pltpu.VMEM((640, D), BF), pltpu.VMEM((640, 2 * D), BF),
    ]
    return attend_call(
        near_kernel, xl, (q, k, v), (q_got, *arrays), outs, [by_head(a) for a in outs], scratch, 12
    )


def attend_far(xl, q, q_got, arrays):
    rows, cols = q.shape[0], q.shape[1] // 2
    outs = [jax.ShapeDtypeStruct((rows, 2 * cols), BF), jax.ShapeDtypeStruct((rows, cols), BF)]
    coarse_n = 4 * arrays[7].shape[1]
    scratch = [
        pltpu.VMEM((704, D), BF), pltpu.VMEM((704, 2 * D), BF),
        pltpu.VMEM((coarse_n, D), BF), pltpu.VMEM((coarse_n, 2 * D), BF),
        pltpu.VMEM((384, D), BF), pltpu.VMEM((384, 2 * D), BF),
        pltpu.VMEM((64, coarse_n), BF),
    ]
    return attend_call(
        far_kernel, xl, (q,), (q_got, *arrays), outs,
        [pl.BlockSpec((rows, D), column(D)), by_head(outs[1])], scratch, 15,
    )


def moved(a, axis, step):
    n = lax.axis_size(axis)
    return lax.ppermute(a, axis, [(i, (i + step) % n) for i in range(n)])


def shifted(a, step):
    n = lax.axis_size(YZ)
    return lax.ppermute(a, YZ, [(i, i + step) for i in range(n) if 0 <= i + step < n])


def round_y(a):
    ny, nz = lax.axis_size("y"), lax.axis_size("z")
    route = []
    for y in range(ny):
        for z in range(nz):
            to = (y + 1 if z < nz // 2 else y + ny - 1) % ny
            route.append((y * nz + z, to * nz + z))
    return lax.ppermute(a, YZ, route)


def per_device(queries, key_rows, value_rows):
    xl = lax.axis_index("xl")
    low = xl == 0
    at = xl.reshape(1)
    half = queries.shape[1] // 2

    def theirs(a):
        return lax.dynamic_slice_in_dim(a, (1 - xl) * half, half, a.ndim - 1)

    def swapped(a):
        return moved(a, "xl", 1)

    unit = coarse_rows(at, key_rows, value_rows)
    unit_got = swapped(unit)
    kv_send = jnp.stack([theirs(key_rows), theirs(value_rows)])
    kv_send, q_send, unit_got = lax.optimization_barrier((kv_send, theirs(queries), unit_got))
    kv_got, q_got = swapped(kv_send), swapped(q_send)
    kept = unit.reshape(2, 8, half)[:, 0:4]
    came = unit_got.reshape(2, 8, half)[:, 4:8]
    unit = jnp.concatenate([jnp.where(low, kept, came), jnp.where(low, came, kept)], axis=1).reshape(16, half)
    units = lax.all_gather(unit, "z")
    units = jnp.moveaxis(units.reshape(-1, 2, 8, half), 1, 0).reshape(2, -1, half)
    kv_got, units, q_got = lax.optimization_barrier((kv_got, units, q_got))
    up1, down1, mid, far = pooled(at, key_rows, value_rows, kv_got)
    below1, above1 = shifted(up1, 1), shifted(down1, -1)
    coarse = [units]
    for _ in range(lax.axis_size("y") - 1):
        coarse.append(round_y(coarse[-1]))
    below3, above3 = shifted(far[:, 96:128], 3), shifted(far[:, 0:32], -3)
    below1, above1, below3, above3 = lax.optimization_barrier((below1, above1, below3, above3))
    up, down, near = forwarded(below1, above1)
    below2, above2 = shifted(up, 1), shifted(down, -1)
    near_out, near_stat = attend_near(
        at, queries, q_got, key_rows, value_rows, (kv_got, mid, below1, above1, near)
    )
    out, send_out = attend_far(
        at, queries, q_got,
        (far, up, down, below2, above2, below3, above3, *coarse, near_out, near_stat),
    )
    return lax.dynamic_update_slice_in_dim(out, swapped(send_out), (1 - xl) * half, 1)


def solution(mesh):
    torus = Mesh(
        mesh.devices.reshape(4, 16, 2, mesh.shape["head"]), ("y", "z", "xl", "head")
    )
    spec = P(SEQ, "head")
    return jax.shard_map(
        per_device, mesh=torus, in_specs=(spec, spec, spec), out_specs=spec, check_vma=False
    )
```

```python
import functools
import math

import jax
import jax.numpy as jnp
from jax import lax
from jax.experimental import pallas as pl
from jax.experimental.pallas import tpu as pltpu
from jax.sharding import Mesh
from jax.sharding import PartitionSpec as P

D = 128
BLOCK = 128
FAR_REACH = 9
SEQ = ("y", "z", "xl")
YZ = ("y", "z")
Z = "z"
BF = jnp.bfloat16
F32 = jnp.float32
SCALE = math.log2(math.e) / math.sqrt(D)
VMEM = pltpu.CompilerParams(vmem_limit_bytes=58 * 2**20)


def taking(microseconds):
    return pl.CostEstimate(flops=0, bytes_accessed=int(microseconds * 3.6e6), transcendentals=0)


def halved(x, scratch):
    rows, cols = x.shape
    parts = []
    for c in range(cols // D):
        scratch[c, 0:rows] = x[:, c * D : (c + 1) * D]
        even = scratch[c, pl.ds(0, rows // 2, stride=2)]
        odd = scratch[c, pl.ds(1, rows // 2, stride=2)]
        parts.append((0.5 * (even + odd)).astype(BF))
    return parts[0] if len(parts) == 1 else jnp.concatenate(parts, axis=1)


def column(width, other=False):
    n = 8 * D // width

    def index(i, xl):
        return (0, (1 - xl[0] if other else xl[0]) * n + i)

    return index


def coarse_kernel(xl, k_own, k_send, v_own, v_send, unit_ref, scratch):
    pieces = []
    for ref in (k_own, k_send, v_own, v_send):
        four = halved(halved(ref[...].astype(F32), scratch).astype(F32), scratch)
        rows, cols = four.shape
        pieces.append(jnp.sum(four.astype(F32).reshape(rows // 16, 16, cols), axis=1) * (1.0 / 16))
    unit_ref[...] = jnp.concatenate(pieces, axis=0).astype(BF)


def coarse_rows(xl, k, v):
    rows, cols = k.shape[0], k.shape[1] // 2
    width = 512
    own, send = (pl.BlockSpec((rows, width), column(width, other)) for other in (False, True))
    return pl.pallas_call(
        coarse_kernel,
        grid_spec=pltpu.PrefetchScalarGridSpec(
            num_scalar_prefetch=1,
            grid=(cols // width,),
            in_specs=[own, send, own, send],
            out_specs=pl.BlockSpec((16, width), lambda c, xl: (0, c)),
            scratch_shapes=[pltpu.VMEM((width // D, rows, D), F32)],
        ),
        out_shape=jax.ShapeDtypeStruct((16, cols), BF),
        compiler_params=VMEM,
        cost_estimate=taking(3),
    )(xl, k, k, v, v)


def pool_kernel(xl, k_ref, v_ref, got_ref, up_ref, down_ref, mid_ref, far_ref, scratch):
    low = xl[0] == 0
    for i, ref in enumerate((k_ref, v_ref)):
        own, got = ref[...], got_ref[i]
        first = jnp.where(low, own, got)
        second = jnp.where(low, got, own)
        mid_first = halved(first.astype(F32), scratch)
        mid_second = halved(second.astype(F32), scratch)
        far_first = halved(mid_first.astype(F32), scratch)
        far_second = halved(mid_second.astype(F32), scratch)
        mid_ref[i, 0:128] = mid_first
        mid_ref[i, 128:256] = mid_second
        far_ref[i, 0:64] = far_first
        far_ref[i, 64:128] = far_second
        up_ref[i, 0:128] = second[128:256]
        up_ref[i, 128:192] = mid_first[64:128]
        up_ref[i, 192:256] = mid_second[0:64]
        up_ref[i, 256:288] = far_first[0:32]
        down_ref[i, 0:128] = first[0:128]
        down_ref[i, 128:192] = mid_first[64:128]
        down_ref[i, 192:256] = mid_second[0:64]
        down_ref[i, 256:288] = far_second[32:64]


def pooled(xl, k, v, got):
    _, rows, cols = got.shape
    width = 256
    sizes = (288, 288, 256, 128)
    own = pl.BlockSpec((rows, width), column(width))
    return pl.pallas_call(
        pool_kernel,
        grid_spec=pltpu.PrefetchScalarGridSpec(
            num_scalar_prefetch=1,
            grid=(cols // width,),
            in_specs=[own, own, pl.BlockSpec((2, rows, width), lambda c, xl: (0, 0, c))],
            out_specs=[pl.BlockSpec((2, n, width), lambda c, xl: (0, 0, c)) for n in sizes],
            scratch_shapes=[pltpu.VMEM((width // D, rows, D), F32)],
        ),
        out_shape=[jax.ShapeDtypeStruct((2, n, cols), BF) for n in sizes],
        compiler_params=VMEM, cost_estimate=taking(5),
    )(xl, k, v, got)


def forward_kernel(below_ref, above_ref, up_ref, down_ref, near_ref, scratch):
    below, above = below_ref[0], above_ref[0]
    below_near = halved(below[0:128].astype(F32), scratch)
    above_near = halved(above[0:128].astype(F32), scratch)
    near_ref[0, 0:64] = below_near
    near_ref[0, 64:128] = above_near
    up_ref[0, 0:32] = below[256:288]
    up_ref[0, 32:128] = halved(jnp.concatenate([below[128:256], below_near], axis=0).astype(F32), scratch)
    down_ref[0, 0:96] = halved(jnp.concatenate([above_near, above[128:256]], axis=0).astype(F32), scratch)
    down_ref[0, 96:128] = above[256:288]


def forwarded(below, above):
    _, rows, cols = below.shape
    width = 512
    return pl.pallas_call(
        forward_kernel,
        grid=(2, cols // width),
        in_specs=[pl.BlockSpec((1, rows, width), lambda i, c: (i, 0, c))] * 2,
        out_specs=[pl.BlockSpec((1, 128, width), lambda i, c: (i, 0, c))] * 3,
        out_shape=[jax.ShapeDtypeStruct((2, 128, cols), BF)] * 3,
        scratch_shapes=[pltpu.VMEM((width // D, 192, D), F32)],
        compiler_params=VMEM, cost_estimate=taking(4),
    )(below, above)


def flags(blocks, first, unit, ref):
    ny, nz = lax.axis_size("y"), lax.axis_size("z")
    at = 4 * (lax.axis_index("y") * nz + lax.axis_index("z"))
    block = first + lax.broadcasted_iota(jnp.int32, (blocks * unit, D), 0) // unit + at
    ref[:, D : 2 * D] = jnp.where((block >= 0) & (block < 4 * ny * nz), 1.0, 0.0).astype(BF)


def present():
    ny, nz = lax.axis_size("y"), lax.axis_size("z")
    zz = lax.axis_index("y") * nz + lax.axis_index("z")
    return [zz >= n for n in range(4)], [zz <= ny * nz - 1 - n for n in range(4)]


def put(ref, start, rows, here, fallback):
    ref[start : start + rows.shape[0], 0:D] = rows if fallback is None else jnp.where(here, rows, fallback)


def scores(q, key):
    return lax.dot_general(q, key, (((1,), (1,)), ((), ())), preferred_element_type=F32)


def weighted(parts, top):
    total = jnp.zeros((BLOCK, 2 * D), F32)
    for s, value, size, keep in parts:
        weights = jnp.exp2(s * SCALE - (top - size)).astype(BF)
        if keep is not None:
            weights = weights * keep
        total = total + jnp.dot(weights, value, preferred_element_type=F32)
    return total


def top_of(parts):
    return functools.reduce(
        jnp.maximum, [jnp.max(s, axis=1, keepdims=True) * SCALE + size for s, _, size, _ in parts]
    )


def near_kernel(xl, q_own, q_got, k_own, v_own, kv_got, mid, below1, above1, near, out, stat, kf, vf, km, vm):
    low = xl[0] == 0

    @pl.when(pl.program_id(0) == 0)
    def _():
        flags(6, -1, 128, vf)
        flags(10, -3, 64, vm)

    has, has_up = present()
    for i, (own_ref, fine_w, mid_w) in enumerate(((k_own, kf, km), (v_own, vf, vm))):
        is_key = i == 0
        own, got = own_ref[...], kv_got[i]
        first, second = jnp.where(low, own, got), jnp.where(low, got, own)
        fine_w[128:384, 0:D] = first
        fine_w[384:640, 0:D] = second
        put(fine_w, 0, below1[i, 0:128], has[1], first[0:128] if is_key else None)
        put(fine_w, 640, above1[i, 0:128], has_up[1], second[128:256] if is_key else None)
        mid_w[192:448, 0:D] = mid[i]
        m0 = mid[i, 0:64] if is_key else None
        m3 = mid[i, 192:256] if is_key else None
        put(mid_w, 0, below1[i, 128:192], has[1], m0)
        put(mid_w, 64, below1[i, 192:256], has[1], m0)
        put(mid_w, 128, near[i, 0:64], has[1], m0)
        put(mid_w, 448, near[i, 64:128], has_up[1], m3)
        put(mid_w, 512, above1[i, 128:192], has_up[1], m3)
        put(mid_w, 576, above1[i, 192:256], has_up[1], m3)
    qo, qg = q_own[...], q_got[...]
    queries = (jnp.where(low, qo, qg), jnp.where(low, qg, qo))
    left = lax.broadcasted_iota(jnp.int32, (BLOCK, D), 1) < D // 2
    for b in range(4):
        q = queries[b // 2][(b % 2) * 128 : (b % 2 + 1) * 128]
        lo, up = b * 64, (b + 5) * 64
        parts = [
            (scores(q, kf[b * 128 : b * 128 + 384]), vf[b * 128 : b * 128 + 384], 0.0, None),
            (scores(q, km[lo : lo + 128]), vm[lo : lo + 128], 1.0, None),
            (scores(q, km[up : up + 128]), vm[up : up + 128], 1.0, None),
        ]
        top = top_of(parts)
        total = weighted(parts, top)
        out[b * 128 : (b + 1) * 128] = total[:, 0:D]
        stat[b * 128 : (b + 1) * 128] = jnp.where(left, top, total[:, D : 2 * D])


def far_kernel(
    xl, q_own, q_got, far, up, down, below2, above2, below3, above3, coarse0, coarse1, coarse2, coarse3, near_out, near_stat,
    own_out, send_out, kr, vr, kc, vc, kfar, vfar, mask,
):
    low = xl[0] == 0
    y = lax.axis_index("y")
    ny, nz = lax.axis_size("y"), lax.axis_size("z")
    coarse_n = 4 * coarse0.shape[1]

    @pl.when(pl.program_id(0) == 0)
    def _():
        flags(22, -9, 32, vr)
        vc[:, D : 2 * D] = jnp.ones((coarse_n, D), BF)
        for b in range(4):
            at = lax.broadcasted_iota(jnp.int32, (16, coarse_n), 1)
            turn = at // (8 * nz)
            other = (y + jnp.where(lax.axis_index("z") < nz // 2, turn, ny - turn)) % ny
            block = (other * nz + (at // 8) % nz) * 4 + (at % 8) // 2
            gap = jnp.abs(block - (4 * (y * nz + lax.axis_index("z")) + b))
            mask[b * 16 : (b + 1) * 16, :] = jnp.where(gap > FAR_REACH, 1.0, 0.0).astype(BF)

    has, has_up = present()
    for i, far_w in enumerate((kr, vr)):
        is_key = i == 0
        far_w[288:416, 0:D] = far[i]
        f0 = far[i, 0:32] if is_key else None
        f3 = far[i, 96:128] if is_key else None
        f0_4 = jnp.concatenate([f0] * 4, axis=0) if is_key else None
        f3_4 = jnp.concatenate([f3] * 4, axis=0) if is_key else None
        put(far_w, 0, below3[i], has[3], f0)
        put(far_w, 32, below2[i], has[2], f0_4)
        put(far_w, 160, up[i], has[1], f0_4)
        put(far_w, 416, down[i], has_up[1], f3_4)
        put(far_w, 544, above2[i], has_up[2], f3_4)
        put(far_w, 672, above3[i], has_up[3], f3)
    step = coarse_n // 4
    for t, part in enumerate((coarse0, coarse1, coarse2, coarse3)):
        kc[t * step : (t + 1) * step] = part[0]
        vc[t * step : (t + 1) * step, 0:D] = part[1]
    qo, qg = q_own[...], q_got[...]
    queries = (jnp.where(low, qo, qg), jnp.where(low, qg, qo))
    results = []
    for b in range(4):
        q = queries[b // 2][(b % 2) * 128 : (b % 2 + 1) * 128]
        kfar[0:192] = kr[b * 32 : b * 32 + 192]
        kfar[192:384] = kr[(b + 13) * 32 : (b + 13) * 32 + 192]
        vfar[0:192] = vr[b * 32 : b * 32 + 192]
        vfar[192:384] = vr[(b + 13) * 32 : (b + 13) * 32 + 192]
        parts = [
            (scores(q, kfar[...]), vfar[...], 2.0, None),
            (scores(q, kc[...]), vc[...], 6.0, mask[b * 16 : b * 16 + 1, :]),
        ]
        here = slice(b * 128, (b + 1) * 128)
        near_top, near_sum = near_stat[here, 0:1], near_stat[here, D - 1 : D]
        top = jnp.maximum(top_of(parts), near_top)
        total = weighted(parts, top)
        scale = jnp.exp2(near_top - top)
        upper = total[:, 0:D] + near_out[here] * scale
        results.append((upper / (total[:, D : 2 * D] + near_sum * scale)).astype(BF))
    out_first = jnp.concatenate(results[0:2], axis=0)
    out_second = jnp.concatenate(results[2:4], axis=0)
    own_out[...] = jnp.where(low, out_first, out_second)
    send_out[...] = jnp.where(low, out_second, out_first)


def by_head(a):
    lead = a.shape[:-1]
    return pl.BlockSpec(lead + (D,), lambda h, xl, n=len(lead): (0,) * n + (h,))


def attend_call(kernel, xl, own, arrays, outs, out_specs, scratch, cost):
    rows, cols = own[0].shape[0], own[0].shape[1] // 2
    spec_own = pl.BlockSpec((rows, D), column(D))
    order = [(own[0], spec_own), (arrays[0], by_head(arrays[0]))]
    order += [(a, spec_own) for a in own[1:]] + [(a, by_head(a)) for a in arrays[1:]]
    return pl.pallas_call(
        kernel,
        grid_spec=pltpu.PrefetchScalarGridSpec(
            num_scalar_prefetch=1,
            grid=(cols // D,),
            in_specs=[spec for _, spec in order],
            out_specs=out_specs,
            scratch_shapes=scratch,
        ),
        out_shape=outs,
        compiler_params=VMEM,
        cost_estimate=taking(cost),
    )(xl, *(a for a, _ in order))


def attend_near(xl, q, q_got, k, v, arrays):
    rows, cols = q.shape[0], q.shape[1] // 2
    outs = [jax.ShapeDtypeStruct((2 * rows, cols), F32)] * 2
    scratch = [
        pltpu.VMEM((768, D), BF), pltpu.VMEM((768, 2 * D), BF),
        pltpu.VMEM((640, D), BF), pltpu.VMEM((640, 2 * D), BF),
    ]
    return attend_call(
        near_kernel, xl, (q, k, v), (q_got, *arrays), outs, [by_head(a) for a in outs], scratch, 12
    )


def attend_far(xl, q, q_got, arrays):
    rows, cols = q.shape[0], q.shape[1] // 2
    outs = [jax.ShapeDtypeStruct((rows, 2 * cols), BF), jax.ShapeDtypeStruct((rows, cols), BF)]
    coarse_n = 4 * arrays[7].shape[1]
    scratch = [
        pltpu.VMEM((704, D), BF), pltpu.VMEM((704, 2 * D), BF),
        pltpu.VMEM((coarse_n, D), BF), pltpu.VMEM((coarse_n, 2 * D), BF),
        pltpu.VMEM((384, D), BF), pltpu.VMEM((384, 2 * D), BF),
        pltpu.VMEM((64, coarse_n), BF),
    ]
    return attend_call(
        far_kernel, xl, (q,), (q_got, *arrays), outs,
        [pl.BlockSpec((rows, D), column(D)), by_head(outs[1])], scratch, 15,
    )


def moved(a, axis, step):
    n = lax.axis_size(axis)
    return lax.ppermute(a, axis, [(i, (i + step) % n) for i in range(n)])


def shifted(a, step):
    n = lax.axis_size(YZ)
    return lax.ppermute(a, YZ, [(i, i + step) for i in range(n) if 0 <= i + step < n])


def round_y(a):
    ny, nz = lax.axis_size("y"), lax.axis_size("z")
    route = []
    for y in range(ny):
        for z in range(nz):
            to = (y + ny - 1 if z < nz // 2 else y + 1) % ny
            route.append((y * nz + z, to * nz + z))
    return lax.ppermute(a, YZ, route)


def per_device(queries, key_rows, value_rows):
    xl = lax.axis_index("xl")
    low = xl == 0
    at = xl.reshape(1)
    half = queries.shape[1] // 2

    def theirs(a):
        return lax.dynamic_slice_in_dim(a, (1 - xl) * half, half, a.ndim - 1)

    def swapped(a):
        return moved(a, "xl", 1)

    unit = coarse_rows(at, key_rows, value_rows)
    unit_got = swapped(unit)
    kv_send = jnp.stack([theirs(key_rows), theirs(value_rows)])
    kv_send, q_send, unit_got = lax.optimization_barrier((kv_send, theirs(queries), unit_got))
    kv_got, q_got = swapped(kv_send), swapped(q_send)
    kept = unit.reshape(2, 8, half)[:, 0:4]
    came = unit_got.reshape(2, 8, half)[:, 4:8]
    unit = jnp.concatenate([jnp.where(low, kept, came), jnp.where(low, came, kept)], axis=1).reshape(16, half)
    units = lax.all_gather(unit, "z")
    units = jnp.moveaxis(units.reshape(-1, 2, 8, half), 1, 0).reshape(2, -1, half)
    kv_got, units, q_got = lax.optimization_barrier((kv_got, units, q_got))
    up1, down1, mid, far = pooled(at, key_rows, value_rows, kv_got)
    below1, above1 = shifted(up1, 1), shifted(down1, -1)
    coarse = [units]
    for _ in range(lax.axis_size("y") - 1):
        coarse.append(round_y(coarse[-1]))
    below3, above3 = shifted(far[:, 96:128], 3), shifted(far[:, 0:32], -3)
    below1, above1, below3, above3 = lax.optimization_barrier((below1, above1, below3, above3))
    up, down, near = forwarded(below1, above1)
    below2, above2 = shifted(up, 1), shifted(down, -1)
    near_out, near_stat = attend_near(
        at, queries, q_got, key_rows, value_rows, (kv_got, mid, below1, above1, near)
    )
    out, send_out = attend_far(
        at, queries, q_got,
        (far, up, down, below2, above2, below3, above3, *coarse, near_out, near_stat),
    )
    return lax.dynamic_update_slice_in_dim(out, swapped(send_out), (1 - xl) * half, 1)


def solution(mesh):
    torus = Mesh(
        mesh.devices.reshape(4, 16, 2, mesh.shape["head"]), ("y", "z", "xl", "head")
    )
    spec = P(SEQ, "head")
    return jax.shard_map(
        per_device, mesh=torus, in_specs=(spec, spec, spec), out_specs=spec, check_vma=False
    )
```

```python
import functools
import math

import jax
import jax.numpy as jnp
from jax import lax
from jax.experimental import pallas as pl
from jax.experimental.pallas import tpu as pltpu
from jax.sharding import Mesh
from jax.sharding import PartitionSpec as P

D = 128
BLOCK = 128
FAR_REACH = 9
SEQ = ("y", "z", "xl")
YZ = ("y", "z")
Z = "z"
BF = jnp.bfloat16
F32 = jnp.float32
SCALE = math.log2(math.e) / math.sqrt(D)
VMEM = pltpu.CompilerParams(vmem_limit_bytes=58 * 2**20)
LITTLE_VMEM = pltpu.CompilerParams(vmem_limit_bytes=24 * 2**20)


def taking(microseconds):
    return pl.CostEstimate(flops=0, bytes_accessed=int(microseconds * 3.6e6), transcendentals=0)


def halved(x, scratch):
    rows, cols = x.shape
    parts = []
    for c in range(cols // D):
        scratch[c, 0:rows] = x[:, c * D : (c + 1) * D]
        even = scratch[c, pl.ds(0, rows // 2, stride=2)]
        odd = scratch[c, pl.ds(1, rows // 2, stride=2)]
        parts.append((0.5 * (even + odd)).astype(BF))
    return parts[0] if len(parts) == 1 else jnp.concatenate(parts, axis=1)


def column(width, other=False):
    n = 8 * D // width

    def index(i, xl):
        return (0, (1 - xl[0] if other else xl[0]) * n + i)

    return index


def coarse_kernel(xl, k_own, k_send, v_own, v_send, unit_ref, scratch):
    pieces = []
    for ref in (k_own, k_send, v_own, v_send):
        four = halved(halved(ref[...].astype(F32), scratch).astype(F32), scratch)
        rows, cols = four.shape
        pieces.append(jnp.sum(four.astype(F32).reshape(rows // 16, 16, cols), axis=1) * (1.0 / 16))
    unit_ref[...] = jnp.concatenate(pieces, axis=0).astype(BF)


def coarse_rows(xl, k, v):
    rows, cols = k.shape[0], k.shape[1] // 2
    width = 512
    own, send = (pl.BlockSpec((rows, width), column(width, other)) for other in (False, True))
    return pl.pallas_call(
        coarse_kernel,
        grid_spec=pltpu.PrefetchScalarGridSpec(
            num_scalar_prefetch=1,
            grid=(cols // width,),
            in_specs=[own, send, own, send],
            out_specs=pl.BlockSpec((16, width), lambda c, xl: (0, c)),
            scratch_shapes=[pltpu.VMEM((width // D, rows, D), F32)],
        ),
        out_shape=jax.ShapeDtypeStruct((16, cols), BF),
        compiler_params=VMEM,
        cost_estimate=taking(3),
    )(xl, k, k, v, v)


def pool_kernel(xl, k_ref, v_ref, got_ref, up_ref, down_ref, mid_ref, far_ref, up3_ref, down3_ref, scratch):
    low = xl[0] == 0
    for i, ref in enumerate((k_ref, v_ref)):
        own, got = ref[...], got_ref[i]
        first = jnp.where(low, own, got)
        second = jnp.where(low, got, own)
        mid_first = halved(first.astype(F32), scratch)
        mid_second = halved(second.astype(F32), scratch)
        far_first = halved(mid_first.astype(F32), scratch)
        far_second = halved(mid_second.astype(F32), scratch)
        mid_ref[i, 0:128] = mid_first
        mid_ref[i, 128:256] = mid_second
        far_ref[i, 0:64] = far_first
        far_ref[i, 64:128] = far_second
        up3_ref[i] = far_second[32:64]
        down3_ref[i] = far_first[0:32]
        up_ref[i, 0:128] = second[128:256]
        up_ref[i, 128:192] = mid_first[64:128]
        up_ref[i, 192:256] = mid_second[0:64]
        up_ref[i, 256:288] = far_first[0:32]
        down_ref[i, 0:128] = first[0:128]
        down_ref[i, 128:192] = mid_first[64:128]
        down_ref[i, 192:256] = mid_second[0:64]
        down_ref[i, 256:288] = far_second[32:64]


def pooled(xl, k, v, got):
    _, rows, cols = got.shape
    width = 256
    sizes = (288, 288, 256, 128, 32, 32)
    own = pl.BlockSpec((rows, width), column(width))
    return pl.pallas_call(
        pool_kernel,
        grid_spec=pltpu.PrefetchScalarGridSpec(
            num_scalar_prefetch=1,
            grid=(cols // width,),
            in_specs=[own, own, pl.BlockSpec((2, rows, width), lambda c, xl: (0, 0, c))],
            out_specs=[pl.BlockSpec((2, n, width), lambda c, xl: (0, 0, c)) for n in sizes],
            scratch_shapes=[pltpu.VMEM((width // D, rows, D), F32)],
        ),
        out_shape=[jax.ShapeDtypeStruct((2, n, cols), BF) for n in sizes],
        compiler_params=VMEM, cost_estimate=taking(5),
    )(xl, k, v, got)


def forward_kernel(below_ref, above_ref, up_ref, down_ref, near_ref, scratch):
    below, above = below_ref[0], above_ref[0]
    below_near = halved(below[0:128].astype(F32), scratch)
    above_near = halved(above[0:128].astype(F32), scratch)
    near_ref[0, 0:64] = below_near
    near_ref[0, 64:128] = above_near
    up_ref[0, 0:32] = below[256:288]
    up_ref[0, 32:128] = halved(jnp.concatenate([below[128:256], below_near], axis=0).astype(F32), scratch)
    down_ref[0, 0:96] = halved(jnp.concatenate([above_near, above[128:256]], axis=0).astype(F32), scratch)
    down_ref[0, 96:128] = above[256:288]


def forwarded(below, above):
    _, rows, cols = below.shape
    width = 512
    return pl.pallas_call(
        forward_kernel,
        grid=(2, cols // width),
        in_specs=[pl.BlockSpec((1, rows, width), lambda i, c: (i, 0, c))] * 2,
        out_specs=[pl.BlockSpec((1, 128, width), lambda i, c: (i, 0, c))] * 3,
        out_shape=[jax.ShapeDtypeStruct((2, 128, cols), BF)] * 3,
        scratch_shapes=[pltpu.VMEM((width // D, 192, D), F32)],
        compiler_params=LITTLE_VMEM, cost_estimate=taking(4),
    )(below, above)


def flags(blocks, first, unit, ref):
    ny, nz = lax.axis_size("y"), lax.axis_size("z")
    at = 4 * (lax.axis_index("y") * nz + lax.axis_index("z"))
    block = first + lax.broadcasted_iota(jnp.int32, (blocks * unit, D), 0) // unit + at
    ref[:, D : 2 * D] = jnp.where((block >= 0) & (block < 4 * ny * nz), 1.0, 0.0).astype(BF)


def present():
    ny, nz = lax.axis_size("y"), lax.axis_size("z")
    zz = lax.axis_index("y") * nz + lax.axis_index("z")
    return [zz >= n for n in range(4)], [zz <= ny * nz - 1 - n for n in range(4)]


def put(ref, start, rows, here, fallback):
    ref[start : start + rows.shape[0], 0:D] = rows if fallback is None else jnp.where(here, rows, fallback)


def scores(q, key):
    return lax.dot_general(q, key, (((1,), (1,)), ((), ())), preferred_element_type=F32)


def weighted(parts, top):
    total = jnp.zeros((BLOCK, 2 * D), F32)
    for s, value, size, keep in parts:
        weights = jnp.exp2(s * SCALE - (top - size)).astype(BF)
        if keep is not None:
            weights = weights * keep
        total = total + jnp.dot(weights, value, preferred_element_type=F32)
    return total


def top_of(parts):
    return functools.reduce(
        jnp.maximum, [jnp.max(s, axis=1, keepdims=True) * SCALE + size for s, _, size, _ in parts]
    )


def near_kernel(xl, q_own, q_got, k_own, v_own, kv_got, mid, below1, above1, near, out, stat, kf, vf, km, vm):
    low = xl[0] == 0

    @pl.when(pl.program_id(0) == 0)
    def _():
        flags(6, -1, 128, vf)
        flags(10, -3, 64, vm)

    has, has_up = present()
    for i, (own_ref, fine_w, mid_w) in enumerate(((k_own, kf, km), (v_own, vf, vm))):
        is_key = i == 0
        own, got = own_ref[...], kv_got[i]
        first, second = jnp.where(low, own, got), jnp.where(low, got, own)
        fine_w[128:384, 0:D] = first
        fine_w[384:640, 0:D] = second
        put(fine_w, 0, below1[i, 0:128], has[1], first[0:128] if is_key else None)
        put(fine_w, 640, above1[i, 0:128], has_up[1], second[128:256] if is_key else None)
        mid_w[192:448, 0:D] = mid[i]
        m0 = mid[i, 0:64] if is_key else None
        m3 = mid[i, 192:256] if is_key else None
        put(mid_w, 0, below1[i, 128:192], has[1], m0)
        put(mid_w, 64, below1[i, 192:256], has[1], m0)
        put(mid_w, 128, near[i, 0:64], has[1], m0)
        put(mid_w, 448, near[i, 64:128], has_up[1], m3)
        put(mid_w, 512, above1[i, 128:192], has_up[1], m3)
        put(mid_w, 576, above1[i, 192:256], has_up[1], m3)
    qo, qg = q_own[...], q_got[...]
    queries = (jnp.where(low, qo, qg), jnp.where(low, qg, qo))
    left = lax.broadcasted_iota(jnp.int32, (BLOCK, D), 1) < D // 2
    for b in range(4):
        q = queries[b // 2][(b % 2) * 128 : (b % 2 + 1) * 128]
        lo, up = b * 64, (b + 5) * 64
        parts = [
            (scores(q, kf[b * 128 : b * 128 + 384]), vf[b * 128 : b * 128 + 384], 0.0, None),
            (scores(q, km[lo : lo + 128]), vm[lo : lo + 128], 1.0, None),
            (scores(q, km[up : up + 128]), vm[up : up + 128], 1.0, None),
        ]
        top = top_of(parts)
        total = weighted(parts, top)
        out[b * 128 : (b + 1) * 128] = total[:, 0:D]
        stat[b * 128 : (b + 1) * 128] = jnp.where(left, top, total[:, D : 2 * D])


def far_kernel(
    xl, q_own, q_got, far, up, down, below2, above2, below3, above3, coarse0, coarse1, coarse2, coarse3, near_out, near_stat,
    own_out, send_out, kr, vr, kc, vc, kfar, vfar, mask,
):
    low = xl[0] == 0
    y = lax.axis_index("y")
    ny, nz = lax.axis_size("y"), lax.axis_size("z")
    coarse_n = 4 * coarse0.shape[1]

    @pl.when(pl.program_id(0) == 0)
    def _():
        flags(22, -9, 32, vr)
        vc[:, D : 2 * D] = jnp.ones((coarse_n, D), BF)
        for b in range(4):
            at = lax.broadcasted_iota(jnp.int32, (16, coarse_n), 1)
            turn = at // (8 * nz)
            other = (y + jnp.where(lax.axis_index("z") < nz // 2, turn, ny - turn)) % ny
            block = (other * nz + (at // 8) % nz) * 4 + (at % 8) // 2
            gap = jnp.abs(block - (4 * (y * nz + lax.axis_index("z")) + b))
            mask[b * 16 : (b + 1) * 16, :] = jnp.where(gap > FAR_REACH, 1.0, 0.0).astype(BF)

    has, has_up = present()
    for i, far_w in enumerate((kr, vr)):
        is_key = i == 0
        far_w[288:416, 0:D] = far[i]
        f0 = far[i, 0:32] if is_key else None
        f3 = far[i, 96:128] if is_key else None
        f0_4 = jnp.concatenate([f0] * 4, axis=0) if is_key else None
        f3_4 = jnp.concatenate([f3] * 4, axis=0) if is_key else None
        put(far_w, 0, below3[i], has[3], f0)
        put(far_w, 32, below2[i], has[2], f0_4)
        put(far_w, 160, up[i], has[1], f0_4)
        put(far_w, 416, down[i], has_up[1], f3_4)
        put(far_w, 544, above2[i], has_up[2], f3_4)
        put(far_w, 672, above3[i], has_up[3], f3)
    step = coarse_n // 4
    for t, part in enumerate((coarse0, coarse1, coarse2, coarse3)):
        kc[t * step : (t + 1) * step] = part[0]
        vc[t * step : (t + 1) * step, 0:D] = part[1]
    qo, qg = q_own[...], q_got[...]
    queries = jnp.concatenate([jnp.where(low, qo, qg), jnp.where(low, qg, qo)], axis=0)
    coarse_scores = scores(queries, kc[...])
    uppers, sums, coarse_weights = [], [], []
    for b in range(4):
        here = slice(b * 128, (b + 1) * 128)
        kfar[0:192] = kr[b * 32 : b * 32 + 192]
        kfar[192:384] = kr[(b + 13) * 32 : (b + 13) * 32 + 192]
        vfar[0:192] = vr[b * 32 : b * 32 + 192]
        vfar[192:384] = vr[(b + 13) * 32 : (b + 13) * 32 + 192]
        fours = (scores(queries[here], kfar[...]), vfar[...], 2.0, None)
        near_top, near_sum = near_stat[here, 0:1], near_stat[here, D - 1 : D]
        top = jnp.maximum(top_of([fours, (coarse_scores[here], None, 6.0, None)]), near_top)
        total = weighted([fours], top)
        scale = jnp.exp2(near_top - top)
        uppers.append(total[:, 0:D] + near_out[here] * scale)
        sums.append(total[:, D : 2 * D] + near_sum * scale)
        weights = jnp.exp2(coarse_scores[here] * SCALE - (top - 6.0)).astype(BF)
        coarse_weights.append(weights * mask[b * 16 : b * 16 + 1, :])
    total = jnp.dot(jnp.concatenate(coarse_weights, axis=0), vc[...], preferred_element_type=F32)
    results = []
    for b in range(4):
        here = slice(b * 128, (b + 1) * 128)
        results.append(((uppers[b] + total[here, 0:D]) / (sums[b] + total[here, D : 2 * D])).astype(BF))
    out_first = jnp.concatenate(results[0:2], axis=0)
    out_second = jnp.concatenate(results[2:4], axis=0)
    own_out[...] = jnp.where(low, out_first, out_second)
    send_out[...] = jnp.where(low, out_second, out_first)


def by_head(a):
    lead = a.shape[:-1]
    return pl.BlockSpec(lead + (D,), lambda h, xl, n=len(lead): (0,) * n + (h,))


def attend_call(kernel, xl, own, arrays, outs, out_specs, scratch, cost):
    rows, cols = own[0].shape[0], own[0].shape[1] // 2
    spec_own = pl.BlockSpec((rows, D), column(D))
    order = [(own[0], spec_own), (arrays[0], by_head(arrays[0]))]
    order += [(a, spec_own) for a in own[1:]] + [(a, by_head(a)) for a in arrays[1:]]
    return pl.pallas_call(
        kernel,
        grid_spec=pltpu.PrefetchScalarGridSpec(
            num_scalar_prefetch=1,
            grid=(cols // D,),
            in_specs=[spec for _, spec in order],
            out_specs=out_specs,
            scratch_shapes=scratch,
        ),
        out_shape=outs,
        compiler_params=VMEM,
        cost_estimate=taking(cost),
    )(xl, *(a for a, _ in order))


def attend_near(xl, q, q_got, k, v, arrays):
    rows, cols = q.shape[0], q.shape[1] // 2
    outs = [jax.ShapeDtypeStruct((2 * rows, cols), F32)] * 2
    scratch = [
        pltpu.VMEM((768, D), BF), pltpu.VMEM((768, 2 * D), BF),
        pltpu.VMEM((640, D), BF), pltpu.VMEM((640, 2 * D), BF),
    ]
    return attend_call(
        near_kernel, xl, (q, k, v), (q_got, *arrays), outs, [by_head(a) for a in outs], scratch, 12
    )


def attend_far(xl, q, q_got, arrays):
    rows, cols = q.shape[0], q.shape[1] // 2
    outs = [jax.ShapeDtypeStruct((rows, 2 * cols), BF), jax.ShapeDtypeStruct((rows, cols), BF)]
    coarse_n = 4 * arrays[7].shape[1]
    scratch = [
        pltpu.VMEM((704, D), BF), pltpu.VMEM((704, 2 * D), BF),
        pltpu.VMEM((coarse_n, D), BF), pltpu.VMEM((coarse_n, 2 * D), BF),
        pltpu.VMEM((384, D), BF), pltpu.VMEM((384, 2 * D), BF),
        pltpu.VMEM((64, coarse_n), BF),
    ]
    return attend_call(
        far_kernel, xl, (q,), (q_got, *arrays), outs,
        [pl.BlockSpec((rows, D), column(D)), by_head(outs[1])], scratch, 15,
    )


def moved(a, axis, step):
    n = lax.axis_size(axis)
    return lax.ppermute(a, axis, [(i, (i + step) % n) for i in range(n)])


def shifted(a, step):
    n = lax.axis_size(YZ)
    return lax.ppermute(a, YZ, [(i, i + step) for i in range(n) if 0 <= i + step < n])


def round_y(a):
    ny, nz = lax.axis_size("y"), lax.axis_size("z")
    route = []
    for y in range(ny):
        for z in range(nz):
            to = (y + ny - 1 if z < nz // 2 else y + 1) % ny
            route.append((y * nz + z, to * nz + z))
    return lax.ppermute(a, YZ, route)


def per_device(queries, key_rows, value_rows):
    xl = lax.axis_index("xl")
    low = xl == 0
    at = xl.reshape(1)
    half = queries.shape[1] // 2

    def theirs(a):
        return lax.dynamic_slice_in_dim(a, (1 - xl) * half, half, a.ndim - 1)

    def swapped(a):
        return moved(a, "xl", 1)

    unit = coarse_rows(at, key_rows, value_rows)
    unit_got = swapped(unit)
    kv_send = jnp.stack([theirs(key_rows), theirs(value_rows)])
    kv_send, q_send, unit_got = lax.optimization_barrier((kv_send, theirs(queries), unit_got))
    kv_got, q_got = swapped(kv_send), swapped(q_send)
    kept = unit.reshape(2, 8, half)[:, 0:4]
    came = unit_got.reshape(2, 8, half)[:, 4:8]
    unit = jnp.concatenate([jnp.where(low, kept, came), jnp.where(low, came, kept)], axis=1).reshape(16, half)
    units = lax.all_gather(unit, "z")
    units = jnp.moveaxis(units.reshape(-1, 2, 8, half), 1, 0).reshape(2, -1, half)
    kv_got, units, q_got = lax.optimization_barrier((kv_got, units, q_got))
    up1, down1, mid, far, up3, down3 = pooled(at, key_rows, value_rows, kv_got)
    below1, above1 = shifted(up1, 1), shifted(down1, -1)
    coarse = [units]
    for _ in range(lax.axis_size("y") - 1):
        coarse.append(round_y(coarse[-1]))
    below3, above3 = shifted(up3, 3), shifted(down3, -3)
    below1, above1, below3, above3 = lax.optimization_barrier((below1, above1, below3, above3))
    up, down, near = forwarded(below1, above1)
    below2, above2 = shifted(up, 1), shifted(down, -1)
    near_out, near_stat = attend_near(
        at, queries, q_got, key_rows, value_rows, (kv_got, mid, below1, above1, near)
    )
    out, send_out = attend_far(
        at, queries, q_got,
        (far, up, down, below2, above2, below3, above3, *coarse, near_out, near_stat),
    )
    return lax.dynamic_update_slice_in_dim(out, swapped(send_out), (1 - xl) * half, 1)


def solution(mesh):
    torus = Mesh(
        mesh.devices.reshape(4, 16, 2, mesh.shape["head"]), ("y", "z", "xl", "head")
    )
    spec = P(SEQ, "head")
    return jax.shard_map(
        per_device, mesh=torus, in_specs=(spec, spec, spec), out_specs=spec, check_vma=False
    )
```

```python
import functools
import math

import jax
import jax.numpy as jnp
from jax import lax
from jax.experimental import pallas as pl
from jax.experimental.pallas import tpu as pltpu
from jax.sharding import Mesh
from jax.sharding import PartitionSpec as P

D = 128
BLOCK = 128
FAR_REACH = 9
SEQ = ("y", "z", "xl")
YZ = ("y", "z")
Z = "z"
BF = jnp.bfloat16
F32 = jnp.float32
SCALE = math.log2(math.e) / math.sqrt(D)
VMEM = pltpu.CompilerParams(vmem_limit_bytes=16 * 2**20)


def taking(microseconds):
    return pl.CostEstimate(flops=0, bytes_accessed=int(microseconds * 3.6e6), transcendentals=0)


def halved(x, scratch):
    rows, cols = x.shape
    parts = []
    for c in range(cols // D):
        scratch[c, 0:rows] = x[:, c * D : (c + 1) * D]
        even = scratch[c, pl.ds(0, rows // 2, stride=2)]
        odd = scratch[c, pl.ds(1, rows // 2, stride=2)]
        parts.append((0.5 * (even + odd)).astype(BF))
    return parts[0] if len(parts) == 1 else jnp.concatenate(parts, axis=1)


def column(width, other=False):
    n = 8 * D // width

    def index(i, xl):
        return (0, (1 - xl[0] if other else xl[0]) * n + i)

    return index


def coarse_kernel(xl, k_own, k_send, v_own, v_send, unit_ref, scratch):
    pieces = []
    for ref in (k_own, k_send, v_own, v_send):
        four = halved(halved(ref[...].astype(F32), scratch).astype(F32), scratch)
        rows, cols = four.shape
        pieces.append(jnp.sum(four.astype(F32).reshape(rows // 16, 16, cols), axis=1) * (1.0 / 16))
    unit_ref[...] = jnp.concatenate(pieces, axis=0).astype(BF)


def coarse_rows(xl, k, v):
    rows, cols = k.shape[0], k.shape[1] // 2
    width = 512
    own, send = (pl.BlockSpec((rows, width), column(width, other)) for other in (False, True))
    return pl.pallas_call(
        coarse_kernel,
        grid_spec=pltpu.PrefetchScalarGridSpec(
            num_scalar_prefetch=1,
            grid=(cols // width,),
            in_specs=[own, send, own, send],
            out_specs=pl.BlockSpec((16, width), lambda c, xl: (0, c)),
            scratch_shapes=[pltpu.VMEM((width // D, rows, D), F32)],
        ),
        out_shape=jax.ShapeDtypeStruct((16, cols), BF),
        compiler_params=VMEM,
        cost_estimate=taking(3),
    )(xl, k, k, v, v)


def pool_kernel(xl, k_ref, v_ref, got_ref, up_ref, down_ref, mid_ref, far_ref, up3_ref, down3_ref, scratch):
    low = xl[0] == 0
    for i, ref in enumerate((k_ref, v_ref)):
        own, got = ref[...], got_ref[i]
        first = jnp.where(low, own, got)
        second = jnp.where(low, got, own)
        mid_first = halved(first.astype(F32), scratch)
        mid_second = halved(second.astype(F32), scratch)
        far_first = halved(mid_first.astype(F32), scratch)
        far_second = halved(mid_second.astype(F32), scratch)
        mid_ref[i, 0:128] = mid_first
        mid_ref[i, 128:256] = mid_second
        far_ref[i, 0:64] = far_first
        far_ref[i, 64:128] = far_second
        up3_ref[i] = far_second[32:64]
        down3_ref[i] = far_first[0:32]
        up_ref[i, 0:128] = second[128:256]
        up_ref[i, 128:192] = mid_first[64:128]
        up_ref[i, 192:256] = mid_second[0:64]
        up_ref[i, 256:288] = far_first[0:32]
        down_ref[i, 0:128] = first[0:128]
        down_ref[i, 128:192] = mid_first[64:128]
        down_ref[i, 192:256] = mid_second[0:64]
        down_ref[i, 256:288] = far_second[32:64]


def pooled(xl, k, v, got):
    _, rows, cols = got.shape
    width = 256
    sizes = (288, 288, 256, 128, 32, 32)
    own = pl.BlockSpec((rows, width), column(width))
    return pl.pallas_call(
        pool_kernel,
        grid_spec=pltpu.PrefetchScalarGridSpec(
            num_scalar_prefetch=1,
            grid=(cols // width,),
            in_specs=[own, own, pl.BlockSpec((2, rows, width), lambda c, xl: (0, 0, c))],
            out_specs=[pl.BlockSpec((2, n, width), lambda c, xl: (0, 0, c)) for n in sizes],
            scratch_shapes=[pltpu.VMEM((width // D, rows, D), F32)],
        ),
        out_shape=[jax.ShapeDtypeStruct((2, n, cols), BF) for n in sizes],
        compiler_params=VMEM, cost_estimate=taking(5),
    )(xl, k, v, got)


def forward_kernel(below_ref, above_ref, up_ref, down_ref, near_ref, scratch):
    below, above = below_ref[0], above_ref[0]
    below_near = halved(below[0:128].astype(F32), scratch)
    above_near = halved(above[0:128].astype(F32), scratch)
    near_ref[0, 0:64] = below_near
    near_ref[0, 64:128] = above_near
    up_ref[0, 0:32] = below[256:288]
    up_ref[0, 32:128] = halved(jnp.concatenate([below[128:256], below_near], axis=0).astype(F32), scratch)
    down_ref[0, 0:96] = halved(jnp.concatenate([above_near, above[128:256]], axis=0).astype(F32), scratch)
    down_ref[0, 96:128] = above[256:288]


def forwarded(below, above):
    _, rows, cols = below.shape
    width = 512
    return pl.pallas_call(
        forward_kernel,
        grid=(2, cols // width),
        in_specs=[pl.BlockSpec((1, rows, width), lambda i, c: (i, 0, c))] * 2,
        out_specs=[pl.BlockSpec((1, 128, width), lambda i, c: (i, 0, c))] * 3,
        out_shape=[jax.ShapeDtypeStruct((2, 128, cols), BF)] * 3,
        scratch_shapes=[pltpu.VMEM((width // D, 192, D), F32)],
        compiler_params=VMEM, cost_estimate=taking(4),
    )(below, above)


def flags(blocks, first, unit, ref):
    ny, nz = lax.axis_size("y"), lax.axis_size("z")
    at = 4 * (lax.axis_index("y") * nz + lax.axis_index("z"))
    block = first + lax.broadcasted_iota(jnp.int32, (blocks * unit, D), 0) // unit + at
    ref[:, D : 2 * D] = jnp.where((block >= 0) & (block < 4 * ny * nz), 1.0, 0.0).astype(BF)


def present():
    ny, nz = lax.axis_size("y"), lax.axis_size("z")
    zz = lax.axis_index("y") * nz + lax.axis_index("z")
    return [zz >= n for n in range(4)], [zz <= ny * nz - 1 - n for n in range(4)]


def put(ref, start, rows, here, fallback):
    ref[start : start + rows.shape[0], 0:D] = rows if fallback is None else jnp.where(here, rows, fallback)


def scores(q, key):
    return lax.dot_general(q, key, (((1,), (1,)), ((), ())), preferred_element_type=F32)


def weighted(parts, top):
    total = jnp.zeros((BLOCK, 2 * D), F32)
    for s, value, size, keep in parts:
        weights = jnp.exp2(s * SCALE - (top - size)).astype(BF)
        if keep is not None:
            weights = weights * keep
        total = total + jnp.dot(weights, value, preferred_element_type=F32)
    return total


def top_of(parts):
    return functools.reduce(
        jnp.maximum, [jnp.max(s, axis=1, keepdims=True) * SCALE + size for s, _, size, _ in parts]
    )


def near_kernel(xl, q_own, q_got, k_own, v_own, kv_got, mid, below1, above1, near, out, stat, kf, vf, km, vm):
    low = xl[0] == 0

    @pl.when(pl.program_id(0) == 0)
    def _():
        flags(6, -1, 128, vf)
        flags(10, -3, 64, vm)

    has, has_up = present()
    for i, (own_ref, fine_w, mid_w) in enumerate(((k_own, kf, km), (v_own, vf, vm))):
        is_key = i == 0
        own, got = own_ref[...], kv_got[i]
        first, second = jnp.where(low, own, got), jnp.where(low, got, own)
        fine_w[128:384, 0:D] = first
        fine_w[384:640, 0:D] = second
        put(fine_w, 0, below1[i, 0:128], has[1], first[0:128] if is_key else None)
        put(fine_w, 640, above1[i, 0:128], has_up[1], second[128:256] if is_key else None)
        mid_w[192:448, 0:D] = mid[i]
        m0 = mid[i, 0:64] if is_key else None
        m3 = mid[i, 192:256] if is_key else None
        put(mid_w, 0, below1[i, 128:192], has[1], m0)
        put(mid_w, 64, below1[i, 192:256], has[1], m0)
        put(mid_w, 128, near[i, 0:64], has[1], m0)
        put(mid_w, 448, near[i, 64:128], has_up[1], m3)
        put(mid_w, 512, above1[i, 128:192], has_up[1], m3)
        put(mid_w, 576, above1[i, 192:256], has_up[1], m3)
    qo, qg = q_own[...], q_got[...]
    queries = (jnp.where(low, qo, qg), jnp.where(low, qg, qo))
    left = lax.broadcasted_iota(jnp.int32, (BLOCK, D), 1) < D // 2
    for b in range(4):
        q = queries[b // 2][(b % 2) * 128 : (b % 2 + 1) * 128]
        lo, up = b * 64, (b + 5) * 64
        parts = [
            (scores(q, kf[b * 128 : b * 128 + 384]), vf[b * 128 : b * 128 + 384], 0.0, None),
            (scores(q, km[lo : lo + 128]), vm[lo : lo + 128], 1.0, None),
            (scores(q, km[up : up + 128]), vm[up : up + 128], 1.0, None),
        ]
        top = top_of(parts)
        total = weighted(parts, top)
        out[b * 128 : (b + 1) * 128] = total[:, 0:D]
        stat[b * 128 : (b + 1) * 128] = jnp.where(left, top, total[:, D : 2 * D])


def far_kernel(
    xl, q_own, q_got, far, up, down, below2, above2, below3, above3, coarse0, coarse1, coarse2, coarse3, near_out, near_stat,
    own_out, send_out, kr, vr, kc, vc, kfar, vfar, mask,
):
    low = xl[0] == 0
    y = lax.axis_index("y")
    ny, nz = lax.axis_size("y"), lax.axis_size("z")
    coarse_n = 4 * coarse0.shape[1]

    @pl.when(pl.program_id(0) == 0)
    def _():
        flags(22, -9, 32, vr)
        vc[:, D : 2 * D] = jnp.ones((coarse_n, D), BF)
        for b in range(4):
            at = lax.broadcasted_iota(jnp.int32, (16, coarse_n), 1)
            turn = at // (8 * nz)
            other = (y + jnp.where(lax.axis_index("z") < nz // 2, turn, ny - turn)) % ny
            block = (other * nz + (at // 8) % nz) * 4 + (at % 8) // 2
            gap = jnp.abs(block - (4 * (y * nz + lax.axis_index("z")) + b))
            mask[b * 16 : (b + 1) * 16, :] = jnp.where(gap > FAR_REACH, 1.0, 0.0).astype(BF)

    has, has_up = present()
    for i, far_w in enumerate((kr, vr)):
        is_key = i == 0
        far_w[288:416, 0:D] = far[i]
        f0 = far[i, 0:32] if is_key else None
        f3 = far[i, 96:128] if is_key else None
        f0_4 = jnp.concatenate([f0] * 4, axis=0) if is_key else None
        f3_4 = jnp.concatenate([f3] * 4, axis=0) if is_key else None
        put(far_w, 0, below3[i], has[3], f0)
        put(far_w, 32, below2[i], has[2], f0_4)
        put(far_w, 160, up[i], has[1], f0_4)
        put(far_w, 416, down[i], has_up[1], f3_4)
        put(far_w, 544, above2[i], has_up[2], f3_4)
        put(far_w, 672, above3[i], has_up[3], f3)
    step = coarse_n // 4
    for t, part in enumerate((coarse0, coarse1, coarse2, coarse3)):
        kc[t * step : (t + 1) * step] = part[0]
        vc[t * step : (t + 1) * step, 0:D] = part[1]
    qo, qg = q_own[...], q_got[...]
    queries = jnp.concatenate([jnp.where(low, qo, qg), jnp.where(low, qg, qo)], axis=0)
    coarse_scores = scores(queries, kc[...])
    uppers, sums, coarse_weights = [], [], []
    for b in range(4):
        here = slice(b * 128, (b + 1) * 128)
        kfar[0:192] = kr[b * 32 : b * 32 + 192]
        kfar[192:384] = kr[(b + 13) * 32 : (b + 13) * 32 + 192]
        vfar[0:192] = vr[b * 32 : b * 32 + 192]
        vfar[192:384] = vr[(b + 13) * 32 : (b + 13) * 32 + 192]
        fours = (scores(queries[here], kfar[...]), vfar[...], 2.0, None)
        near_top, near_sum = near_stat[here, 0:1], near_stat[here, D - 1 : D]
        top = jnp.maximum(top_of([fours, (coarse_scores[here], None, 6.0, None)]), near_top)
        total = weighted([fours], top)
        scale = jnp.exp2(near_top - top)
        uppers.append(total[:, 0:D] + near_out[here] * scale)
        sums.append(total[:, D : 2 * D] + near_sum * scale)
        weights = jnp.exp2(coarse_scores[here] * SCALE - (top - 6.0)).astype(BF)
        coarse_weights.append(weights * mask[b * 16 : b * 16 + 1, :])
    total = jnp.dot(jnp.concatenate(coarse_weights, axis=0), vc[...], preferred_element_type=F32)
    results = []
    for b in range(4):
        here = slice(b * 128, (b + 1) * 128)
        results.append(((uppers[b] + total[here, 0:D]) / (sums[b] + total[here, D : 2 * D])).astype(BF))
    out_first = jnp.concatenate(results[0:2], axis=0)
    out_second = jnp.concatenate(results[2:4], axis=0)
    own_out[...] = jnp.where(low, out_first, out_second)
    send_out[...] = jnp.where(low, out_second, out_first)


def by_head(a):
    lead = a.shape[:-1]
    return pl.BlockSpec(lead + (D,), lambda h, xl, n=len(lead): (0,) * n + (h,))


def attend_call(kernel, xl, own, arrays, outs, out_specs, scratch, cost):
    rows, cols = own[0].shape[0], own[0].shape[1] // 2
    spec_own = pl.BlockSpec((rows, D), column(D))
    order = [(own[0], spec_own), (arrays[0], by_head(arrays[0]))]
    order += [(a, spec_own) for a in own[1:]] + [(a, by_head(a)) for a in arrays[1:]]
    return pl.pallas_call(
        kernel,
        grid_spec=pltpu.PrefetchScalarGridSpec(
            num_scalar_prefetch=1,
            grid=(cols // D,),
            in_specs=[spec for _, spec in order],
            out_specs=out_specs,
            scratch_shapes=scratch,
        ),
        out_shape=outs,
        compiler_params=VMEM,
        cost_estimate=taking(cost),
    )(xl, *(a for a, _ in order))


def attend_near(xl, q, q_got, k, v, arrays):
    rows, cols = q.shape[0], q.shape[1] // 2
    outs = [jax.ShapeDtypeStruct((2 * rows, cols), F32)] * 2
    scratch = [
        pltpu.VMEM((768, D), BF), pltpu.VMEM((768, 2 * D), BF),
        pltpu.VMEM((640, D), BF), pltpu.VMEM((640, 2 * D), BF),
    ]
    return attend_call(
        near_kernel, xl, (q, k, v), (q_got, *arrays), outs, [by_head(a) for a in outs], scratch, 12
    )


def attend_far(xl, q, q_got, arrays):
    rows, cols = q.shape[0], q.shape[1] // 2
    outs = [jax.ShapeDtypeStruct((rows, 2 * cols), BF), jax.ShapeDtypeStruct((rows, cols), BF)]
    coarse_n = 4 * arrays[7].shape[1]
    scratch = [
        pltpu.VMEM((704, D), BF), pltpu.VMEM((704, 2 * D), BF),
        pltpu.VMEM((coarse_n, D), BF), pltpu.VMEM((coarse_n, 2 * D), BF),
        pltpu.VMEM((384, D), BF), pltpu.VMEM((384, 2 * D), BF),
        pltpu.VMEM((64, coarse_n), BF),
    ]
    return attend_call(
        far_kernel, xl, (q,), (q_got, *arrays), outs,
        [pl.BlockSpec((rows, D), column(D)), by_head(outs[1])], scratch, 15,
    )


def moved(a, axis, step):
    n = lax.axis_size(axis)
    return lax.ppermute(a, axis, [(i, (i + step) % n) for i in range(n)])


def shifted(a, step):
    n = lax.axis_size(YZ)
    return lax.ppermute(a, YZ, [(i, i + step) for i in range(n) if 0 <= i + step < n])


def round_y(a):
    ny, nz = lax.axis_size("y"), lax.axis_size("z")
    route = []
    for y in range(ny):
        for z in range(nz):
            to = (y + ny - 1 if z < nz // 2 else y + 1) % ny
            route.append((y * nz + z, to * nz + z))
    return lax.ppermute(a, YZ, route)


def per_device(queries, key_rows, value_rows):
    xl = lax.axis_index("xl")
    low = xl == 0
    at = xl.reshape(1)
    half = queries.shape[1] // 2

    def theirs(a):
        return lax.dynamic_slice_in_dim(a, (1 - xl) * half, half, a.ndim - 1)

    def swapped(a):
        return moved(a, "xl", 1)

    unit = coarse_rows(at, key_rows, value_rows)
    unit_got = swapped(unit)
    kv_send = jnp.stack([theirs(key_rows), theirs(value_rows)])
    kv_send, q_send, unit_got = lax.optimization_barrier((kv_send, theirs(queries), unit_got))
    kv_got, q_got = swapped(kv_send), swapped(q_send)
    kept = unit.reshape(2, 8, half)[:, 0:4]
    came = unit_got.reshape(2, 8, half)[:, 4:8]
    unit = jnp.concatenate([jnp.where(low, kept, came), jnp.where(low, came, kept)], axis=1).reshape(16, half)
    units = lax.all_gather(unit, "z")
    units = jnp.moveaxis(units.reshape(-1, 2, 8, half), 1, 0).reshape(2, -1, half)
    kv_got, units, q_got = lax.optimization_barrier((kv_got, units, q_got))
    up1, down1, mid, far, up3, down3 = pooled(at, key_rows, value_rows, kv_got)
    below1, above1 = shifted(up1, 1), shifted(down1, -1)
    coarse = [units]
    for _ in range(lax.axis_size("y") - 1):
        coarse.append(round_y(coarse[-1]))
    below3, above3 = shifted(up3, 3), shifted(down3, -3)
    below1, above1, below3, above3 = lax.optimization_barrier((below1, above1, below3, above3))
    up, down, near = forwarded(below1, above1)
    below2, above2 = shifted(up, 1), shifted(down, -1)
    near_out, near_stat = attend_near(
        at, queries, q_got, key_rows, value_rows, (kv_got, mid, below1, above1, near)
    )
    out, send_out = attend_far(
        at, queries, q_got,
        (far, up, down, below2, above2, below3, above3, *coarse, near_out, near_stat),
    )
    return lax.dynamic_update_slice_in_dim(out, swapped(send_out), (1 - xl) * half, 1)


def solution(mesh):
    torus = Mesh(
        mesh.devices.reshape(4, 16, 2, mesh.shape["head"]), ("y", "z", "xl", "head")
    )
    spec = P(SEQ, "head")
    return jax.shard_map(
        per_device, mesh=torus, in_specs=(spec, spec, spec), out_specs=spec, check_vma=False
    )
```

```python
import functools
import math

import jax
import jax.numpy as jnp
from jax import lax
from jax.experimental import pallas as pl
from jax.experimental.pallas import tpu as pltpu
from jax.sharding import Mesh
from jax.sharding import PartitionSpec as P

D = 128
BLOCK = 128
FAR_REACH = 9
SEQ = ("y", "z", "xl")
YZ = ("y", "z")
Z = "z"
BF = jnp.bfloat16
F32 = jnp.float32
SCALE = math.log2(math.e) / math.sqrt(D)
VMEM = pltpu.CompilerParams(vmem_limit_bytes=16 * 2**20)


def taking(microseconds):
    return pl.CostEstimate(flops=0, bytes_accessed=int(microseconds * 3.6e6), transcendentals=0)


def halved(x, scratch):
    rows, cols = x.shape
    parts = []
    for c in range(cols // D):
        scratch[c, 0:rows] = x[:, c * D : (c + 1) * D]
        even = scratch[c, pl.ds(0, rows // 2, stride=2)]
        odd = scratch[c, pl.ds(1, rows // 2, stride=2)]
        parts.append((0.5 * (even + odd)).astype(BF))
    return parts[0] if len(parts) == 1 else jnp.concatenate(parts, axis=1)


def column(width, other=False):
    n = 8 * D // width

    def index(i, xl):
        return (0, (1 - xl[0] if other else xl[0]) * n + i)

    return index


def coarse_kernel(xl, k_own, k_send, v_own, v_send, unit_ref, scratch):
    pieces = []
    for ref in (k_own, k_send, v_own, v_send):
        four = halved(halved(ref[...].astype(F32), scratch).astype(F32), scratch)
        rows, cols = four.shape
        pieces.append(jnp.sum(four.astype(F32).reshape(rows // 16, 16, cols), axis=1) * (1.0 / 16))
    unit_ref[...] = jnp.concatenate(pieces, axis=0).astype(BF)


def coarse_rows(xl, k, v):
    rows, cols = k.shape[0], k.shape[1] // 2
    width = 512
    own, send = (pl.BlockSpec((rows, width), column(width, other)) for other in (False, True))
    return pl.pallas_call(
        coarse_kernel,
        grid_spec=pltpu.PrefetchScalarGridSpec(
            num_scalar_prefetch=1,
            grid=(cols // width,),
            in_specs=[own, send, own, send],
            out_specs=pl.BlockSpec((16, width), lambda c, xl: (0, c)),
            scratch_shapes=[pltpu.VMEM((width // D, rows, D), F32)],
        ),
        out_shape=jax.ShapeDtypeStruct((16, cols), BF),
        compiler_params=VMEM,
        cost_estimate=taking(3),
    )(xl, k, k, v, v)


def pool_kernel(xl, k_ref, v_ref, got_ref, up_ref, down_ref, mid_ref, far_ref, up3_ref, down3_ref, scratch):
    low = xl[0] == 0
    for i, ref in enumerate((k_ref, v_ref)):
        own, got = ref[...], got_ref[i]
        first = jnp.where(low, own, got)
        second = jnp.where(low, got, own)
        mid_first = halved(first.astype(F32), scratch)
        mid_second = halved(second.astype(F32), scratch)
        far_first = halved(mid_first.astype(F32), scratch)
        far_second = halved(mid_second.astype(F32), scratch)
        mid_ref[i, 0:128] = mid_first
        mid_ref[i, 128:256] = mid_second
        far_ref[i, 0:64] = far_first
        far_ref[i, 64:128] = far_second
        up3_ref[i] = far_second[32:64]
        down3_ref[i] = far_first[0:32]
        up_ref[i, 0:128] = second[128:256]
        up_ref[i, 128:192] = mid_first[64:128]
        up_ref[i, 192:256] = mid_second[0:64]
        up_ref[i, 256:288] = far_first[0:32]
        down_ref[i, 0:128] = first[0:128]
        down_ref[i, 128:192] = mid_first[64:128]
        down_ref[i, 192:256] = mid_second[0:64]
        down_ref[i, 256:288] = far_second[32:64]


def pooled(xl, k, v, got):
    _, rows, cols = got.shape
    width = 256
    sizes = (288, 288, 256, 128, 32, 32)
    own = pl.BlockSpec((rows, width), column(width))
    return pl.pallas_call(
        pool_kernel,
        grid_spec=pltpu.PrefetchScalarGridSpec(
            num_scalar_prefetch=1,
            grid=(cols // width,),
            in_specs=[own, own, pl.BlockSpec((2, rows, width), lambda c, xl: (0, 0, c))],
            out_specs=[pl.BlockSpec((2, n, width), lambda c, xl: (0, 0, c)) for n in sizes],
            scratch_shapes=[pltpu.VMEM((width // D, rows, D), F32)],
        ),
        out_shape=[jax.ShapeDtypeStruct((2, n, cols), BF) for n in sizes],
        compiler_params=VMEM, cost_estimate=taking(5),
    )(xl, k, v, got)


def forward_kernel(below_ref, above_ref, up_ref, down_ref, near_ref, scratch):
    below, above = below_ref[0], above_ref[0]
    below_near = halved(below[0:128].astype(F32), scratch)
    above_near = halved(above[0:128].astype(F32), scratch)
    near_ref[0, 0:64] = below_near
    near_ref[0, 64:128] = above_near
    up_ref[0, 0:32] = below[256:288]
    up_ref[0, 32:128] = halved(jnp.concatenate([below[128:256], below_near], axis=0).astype(F32), scratch)
    down_ref[0, 0:96] = halved(jnp.concatenate([above_near, above[128:256]], axis=0).astype(F32), scratch)
    down_ref[0, 96:128] = above[256:288]


def forwarded(below, above):
    _, rows, cols = below.shape
    width = 512
    return pl.pallas_call(
        forward_kernel,
        grid=(2, cols // width),
        in_specs=[pl.BlockSpec((1, rows, width), lambda i, c: (i, 0, c))] * 2,
        out_specs=[pl.BlockSpec((1, 128, width), lambda i, c: (i, 0, c))] * 3,
        out_shape=[jax.ShapeDtypeStruct((2, 128, cols), BF)] * 3,
        scratch_shapes=[pltpu.VMEM((width // D, 192, D), F32)],
        compiler_params=VMEM, cost_estimate=taking(4),
    )(below, above)


def flags(blocks, first, unit, ref):
    ny, nz = lax.axis_size("y"), lax.axis_size("z")
    at = 4 * (lax.axis_index("y") * nz + lax.axis_index("z"))
    block = first + lax.broadcasted_iota(jnp.int32, (blocks * unit, D), 0) // unit + at
    ref[:, D : 2 * D] = jnp.where((block >= 0) & (block < 4 * ny * nz), 1.0, 0.0).astype(BF)


def present():
    ny, nz = lax.axis_size("y"), lax.axis_size("z")
    zz = lax.axis_index("y") * nz + lax.axis_index("z")
    return [zz >= n for n in range(4)], [zz <= ny * nz - 1 - n for n in range(4)]


def put(ref, start, rows, here, fallback):
    ref[start : start + rows.shape[0], 0:D] = rows if fallback is None else jnp.where(here, rows, fallback)


def scores(q, key):
    return lax.dot_general(q, key, (((1,), (1,)), ((), ())), preferred_element_type=F32)


def weighted(parts, top):
    total = jnp.zeros((BLOCK, 2 * D), F32)
    for s, value, size, keep in parts:
        weights = jnp.exp2(s * SCALE - (top - size)).astype(BF)
        if keep is not None:
            weights = weights * keep
        total = total + jnp.dot(weights, value, preferred_element_type=F32)
    return total


def top_of(parts):
    return functools.reduce(
        jnp.maximum, [jnp.max(s, axis=1, keepdims=True) * SCALE + size for s, _, size, _ in parts]
    )


def near_kernel(xl, q_own, q_got, k_own, v_own, kv_got, mid, below1, above1, near, out, stat, kf, vf, km, vm):
    low = xl[0] == 0

    @pl.when(pl.program_id(0) == 0)
    def _():
        flags(6, -1, 128, vf)
        flags(10, -3, 64, vm)

    has, has_up = present()
    for i, (own_ref, fine_w, mid_w) in enumerate(((k_own, kf, km), (v_own, vf, vm))):
        is_key = i == 0
        own, got = own_ref[...], kv_got[i]
        first, second = jnp.where(low, own, got), jnp.where(low, got, own)
        fine_w[128:384, 0:D] = first
        fine_w[384:640, 0:D] = second
        put(fine_w, 0, below1[i, 0:128], has[1], first[0:128] if is_key else None)
        put(fine_w, 640, above1[i, 0:128], has_up[1], second[128:256] if is_key else None)
        mid_w[192:448, 0:D] = mid[i]
        m0 = mid[i, 0:64] if is_key else None
        m3 = mid[i, 192:256] if is_key else None
        put(mid_w, 0, below1[i, 128:192], has[1], m0)
        put(mid_w, 64, below1[i, 192:256], has[1], m0)
        put(mid_w, 128, near[i, 0:64], has[1], m0)
        put(mid_w, 448, near[i, 64:128], has_up[1], m3)
        put(mid_w, 512, above1[i, 128:192], has_up[1], m3)
        put(mid_w, 576, above1[i, 192:256], has_up[1], m3)
    qo, qg = q_own[...], q_got[...]
    queries = (jnp.where(low, qo, qg), jnp.where(low, qg, qo))
    left = lax.broadcasted_iota(jnp.int32, (BLOCK, D), 1) < D // 2
    for b in range(4):
        q = queries[b // 2][(b % 2) * 128 : (b % 2 + 1) * 128]
        lo, up = b * 64, (b + 5) * 64
        parts = [
            (scores(q, kf[b * 128 : b * 128 + 384]), vf[b * 128 : b * 128 + 384], 0.0, None),
            (scores(q, km[lo : lo + 128]), vm[lo : lo + 128], 1.0, None),
            (scores(q, km[up : up + 128]), vm[up : up + 128], 1.0, None),
        ]
        top = top_of(parts)
        total = weighted(parts, top)
        out[b * 128 : (b + 1) * 128] = total[:, 0:D]
        stat[b * 128 : (b + 1) * 128] = jnp.where(left, top, total[:, D : 2 * D])


def far_kernel(
    xl, q_own, q_got, far, up, down, below2, above2, below3, above3, coarse0, coarse1, coarse2, coarse3, near_out, near_stat,
    own_out, send_out, kr, vr, kc, vc, kfar, vfar, mask,
):
    low = xl[0] == 0
    y = lax.axis_index("y")
    ny, nz = lax.axis_size("y"), lax.axis_size("z")
    coarse_n = 4 * coarse0.shape[1]

    @pl.when(pl.program_id(0) == 0)
    def _():
        flags(22, -9, 32, vr)
        vc[:, D : 2 * D] = jnp.ones((coarse_n, D), BF)
        for b in range(4):
            at = lax.broadcasted_iota(jnp.int32, (16, coarse_n), 1)
            turn = at // (8 * nz)
            other = (y + jnp.where(lax.axis_index("z") < nz // 2, turn, ny - turn)) % ny
            block = (other * nz + (at // 8) % nz) * 4 + (at % 8) // 2
            gap = jnp.abs(block - (4 * (y * nz + lax.axis_index("z")) + b))
            mask[b * 16 : (b + 1) * 16, :] = jnp.where(gap > FAR_REACH, 1.0, 0.0).astype(BF)

    has, has_up = present()
    for i, far_w in enumerate((kr, vr)):
        is_key = i == 0
        far_w[288:416, 0:D] = far[i]
        f0 = far[i, 0:32] if is_key else None
        f3 = far[i, 96:128] if is_key else None
        f0_4 = jnp.concatenate([f0] * 4, axis=0) if is_key else None
        f3_4 = jnp.concatenate([f3] * 4, axis=0) if is_key else None
        put(far_w, 0, below3[i], has[3], f0)
        put(far_w, 32, below2[i], has[2], f0_4)
        put(far_w, 160, up[i], has[1], f0_4)
        put(far_w, 416, down[i], has_up[1], f3_4)
        put(far_w, 544, above2[i], has_up[2], f3_4)
        put(far_w, 672, above3[i], has_up[3], f3)
    step = coarse_n // 4
    for t, part in enumerate((coarse0, coarse1, coarse2, coarse3)):
        kc[t * step : (t + 1) * step] = part[0]
        vc[t * step : (t + 1) * step, 0:D] = part[1]
    qo, qg = q_own[...], q_got[...]
    queries = (jnp.where(low, qo, qg), jnp.where(low, qg, qo))
    results = []
    for b in range(4):
        q = queries[b // 2][(b % 2) * 128 : (b % 2 + 1) * 128]
        kfar[0:192] = kr[b * 32 : b * 32 + 192]
        kfar[192:384] = kr[(b + 13) * 32 : (b + 13) * 32 + 192]
        vfar[0:192] = vr[b * 32 : b * 32 + 192]
        vfar[192:384] = vr[(b + 13) * 32 : (b + 13) * 32 + 192]
        parts = [
            (scores(q, kfar[...]), vfar[...], 2.0, None),
            (scores(q, kc[...]), vc[...], 6.0, mask[b * 16 : b * 16 + 1, :]),
        ]
        here = slice(b * 128, (b + 1) * 128)
        near_top, near_sum = near_stat[here, 0:1], near_stat[here, D - 1 : D]
        top = jnp.maximum(top_of(parts), near_top)
        total = weighted(parts, top)
        scale = jnp.exp2(near_top - top)
        upper = total[:, 0:D] + near_out[here] * scale
        results.append((upper / (total[:, D : 2 * D] + near_sum * scale)).astype(BF))
    out_first = jnp.concatenate(results[0:2], axis=0)
    out_second = jnp.concatenate(results[2:4], axis=0)
    own_out[...] = jnp.where(low, out_first, out_second)
    send_out[...] = jnp.where(low, out_second, out_first)


def by_head(a):
    lead = a.shape[:-1]
    return pl.BlockSpec(lead + (D,), lambda h, xl, n=len(lead): (0,) * n + (h,))


def attend_call(kernel, xl, own, arrays, outs, out_specs, scratch, cost):
    rows, cols = own[0].shape[0], own[0].shape[1] // 2
    spec_own = pl.BlockSpec((rows, D), column(D))
    order = [(own[0], spec_own), (arrays[0], by_head(arrays[0]))]
    order += [(a, spec_own) for a in own[1:]] + [(a, by_head(a)) for a in arrays[1:]]
    return pl.pallas_call(
        kernel,
        grid_spec=pltpu.PrefetchScalarGridSpec(
            num_scalar_prefetch=1,
            grid=(cols // D,),
            in_specs=[spec for _, spec in order],
            out_specs=out_specs,
            scratch_shapes=scratch,
        ),
        out_shape=outs,
        compiler_params=VMEM,
        cost_estimate=taking(cost),
    )(xl, *(a for a, _ in order))


def attend_near(xl, q, q_got, k, v, arrays):
    rows, cols = q.shape[0], q.shape[1] // 2
    outs = [jax.ShapeDtypeStruct((2 * rows, cols), F32)] * 2
    scratch = [
        pltpu.VMEM((768, D), BF), pltpu.VMEM((768, 2 * D), BF),
        pltpu.VMEM((640, D), BF), pltpu.VMEM((640, 2 * D), BF),
    ]
    return attend_call(
        near_kernel, xl, (q, k, v), (q_got, *arrays), outs, [by_head(a) for a in outs], scratch, 12
    )


def attend_far(xl, q, q_got, arrays):
    rows, cols = q.shape[0], q.shape[1] // 2
    outs = [jax.ShapeDtypeStruct((rows, 2 * cols), BF), jax.ShapeDtypeStruct((rows, cols), BF)]
    coarse_n = 4 * arrays[7].shape[1]
    scratch = [
        pltpu.VMEM((704, D), BF), pltpu.VMEM((704, 2 * D), BF),
        pltpu.VMEM((coarse_n, D), BF), pltpu.VMEM((coarse_n, 2 * D), BF),
        pltpu.VMEM((384, D), BF), pltpu.VMEM((384, 2 * D), BF),
        pltpu.VMEM((64, coarse_n), BF),
    ]
    return attend_call(
        far_kernel, xl, (q,), (q_got, *arrays), outs,
        [pl.BlockSpec((rows, D), column(D)), by_head(outs[1])], scratch, 15,
    )


def moved(a, axis, step):
    n = lax.axis_size(axis)
    return lax.ppermute(a, axis, [(i, (i + step) % n) for i in range(n)])


def shifted(a, step):
    n = lax.axis_size(YZ)
    return lax.ppermute(a, YZ, [(i, i + step) for i in range(n) if 0 <= i + step < n])


def round_y(a):
    ny, nz = lax.axis_size("y"), lax.axis_size("z")
    route = []
    for y in range(ny):
        for z in range(nz):
            to = (y + ny - 1 if z < nz // 2 else y + 1) % ny
            route.append((y * nz + z, to * nz + z))
    return lax.ppermute(a, YZ, route)


def per_device(queries, key_rows, value_rows):
    xl = lax.axis_index("xl")
    low = xl == 0
    at = xl.reshape(1)
    half = queries.shape[1] // 2

    def theirs(a):
        return lax.dynamic_slice_in_dim(a, (1 - xl) * half, half, a.ndim - 1)

    def swapped(a):
        return moved(a, "xl", 1)

    unit = coarse_rows(at, key_rows, value_rows)
    unit_got = swapped(unit)
    kv_send = jnp.stack([theirs(key_rows), theirs(value_rows)])
    kv_send, q_send, unit_got = lax.optimization_barrier((kv_send, theirs(queries), unit_got))
    kv_got, q_got = swapped(kv_send), swapped(q_send)
    kept = unit.reshape(2, 8, half)[:, 0:4]
    came = unit_got.reshape(2, 8, half)[:, 4:8]
    unit = jnp.concatenate([jnp.where(low, kept, came), jnp.where(low, came, kept)], axis=1).reshape(16, half)
    units = lax.all_gather(unit, "z")
    units = jnp.moveaxis(units.reshape(-1, 2, 8, half), 1, 0).reshape(2, -1, half)
    kv_got, units, q_got = lax.optimization_barrier((kv_got, units, q_got))
    up1, down1, mid, far, up3, down3 = pooled(at, key_rows, value_rows, kv_got)
    below1, above1 = shifted(up1, 1), shifted(down1, -1)
    coarse = [units]
    for _ in range(lax.axis_size("y") - 1):
        coarse.append(round_y(coarse[-1]))
    below3, above3 = shifted(up3, 3), shifted(down3, -3)
    below1, above1, below3, above3 = lax.optimization_barrier((below1, above1, below3, above3))
    up, down, near = forwarded(below1, above1)
    below2, above2 = shifted(up, 1), shifted(down, -1)
    near_out, near_stat = attend_near(
        at, queries, q_got, key_rows, value_rows, (kv_got, mid, below1, above1, near)
    )
    out, send_out = attend_far(
        at, queries, q_got,
        (far, up, down, below2, above2, below3, above3, *coarse, near_out, near_stat),
    )
    return lax.dynamic_update_slice_in_dim(out, swapped(send_out), (1 - xl) * half, 1)


def solution(mesh):
    torus = Mesh(
        mesh.devices.reshape(4, 16, 2, mesh.shape["head"]), ("y", "z", "xl", "head")
    )
    spec = P(SEQ, "head")
    return jax.shard_map(
        per_device, mesh=torus, in_specs=(spec, spec, spec), out_specs=spec, check_vma=False
    )
```
